32 devices in a mesh: row: 8 (over y, x, core), col: 4 (over z).
Axes of the slice: x: 2, y: 2, z: 4, core: 2. Of those that a mesh axis runs over, the one named last changes fastest.
Arguments:
- queries: bfloat16 [1024, 2048], P('row', 'col'), may hold values from -48 to 48
- suffix_cache: bfloat16 [1024, 2048], P('row', 'col'), may hold values from -1.875 to 1.875
- suffix_leaf: int32 [8, 128], P('row'), may hold values from 0 to 31, never falling along the last dimension, each value on 1 to 8 neighbouring positions
- leaf_parent: int32 [8, 32], P('row'), may hold values from 0 to 7, as said below
- root_cache: bfloat16 [4096, 2048], P(('row', 'col')), may hold values from -2 to 2
- branch_cache: bfloat16 [8, 8192, 2048], P('row', 'col'), may hold values from -1.875 to 1.875
- branch_length: int32 [8], P('row'), may hold values from 1 to 8192, 49152 in all
- leaf_cache: bfloat16 [256, 256, 2048], P('row', 'col'), may hold values from -1.875 to 1.875
- leaf_length: int32 [256], P('row'), may hold values from 1 to 256, 32768 in all
Outputs:
- attention_out: bfloat16 [1024, 2048], P('row', 'col')
The draws below stay inside these ranges and needn't reach their ends.
Inputs may be any that keep to these rules, and one draw needn't show every extreme that they name: `suffix_leaf`: never falls along a row's tokens; each of the 32 leaves has 1 to 8 tokens. `leaf_parent`: in each row index every branch node is the parent of exactly 4 of its leaves, so at most 32 of that row's tokens lie under one branch node.
All inputs are finite; a program needn't handle non-finite values. No bound on the sum of `branch_length` or of `leaf_length` on one device may be relied on, other than what follows from the above.
Results may differ from the reference program's by a relative error of at most 0.0065.
Values may be sent and summed in bfloat16 or wider, within the bound.
A program may use at most 128 MiB of HBM per device.

```python
import math
import jax
import jax.numpy as jnp
import numpy as np
from jax import lax

HEADS = 8
KV_HEADS = 4
HEAD_DIM = 256
TOK_ROW = 128
LEAF_ROW = 32
ROOT_LEN = 4096
BRANCH_LEN = 8192
LEAF_LEN = 256
QDIM = 2048
KVDIM = 2048
TOKENS = 1024
BRANCHES = 8
LEAVES = 256
MOST = 8
CAP = 32
N_ROW = 8


def root_base(key):
    own_key = jax.random.fold_in(key, 7)
    values = 0.75 * jnp.clip(jax.random.normal(own_key, (ROOT_LEN, KVDIM), jnp.float32), -2.5, 2.5)
    return values


def root_drawn(key):
    values = root_base(key)
    return values


def draw_root_cache(key, part):
    return root_drawn(key).astype(jnp.bfloat16)


def draw_queries(key, part):
    own_key = jax.random.fold_in(key, 3)
    values = 3.4 * jnp.clip(jax.random.normal(own_key, (TOKENS, QDIM), jnp.float32), -6.0, 6.0)
    return values.astype(jnp.bfloat16)


def draw_leaf_parent(key, part):
    own_key = jax.random.fold_in(key, 5)
    row_keys = jax.random.split(own_key, BRANCHES)
    orders = jax.vmap(lambda row_key: jax.random.permutation(row_key, BRANCHES))(row_keys)
    columns = jnp.arange(LEAF_ROW) % BRANCHES
    return orders[:, columns].astype(jnp.int32)


def levels(rng, shape, cuts, low, top_value):
    def one(position, blocks):
        draws = jax.random.uniform(jax.random.fold_in(jax.random.fold_in(rng, 6), position), (blocks,), jnp.float32, low / len(cuts), top_value / len(cuts))
        return jnp.repeat(jnp.exp(draws), shape[position] // blocks).reshape((-1,) + (1,) * (len(shape) - position - 1))

    loudness = one(*cuts[0])
    for cut in cuts[1:]:
        loudness = loudness * one(*cut)
    return loudness


def split_up(amount, total, bound, lean):
    portions = [(1 << 20) // math.isqrt(standing ** lean) + 1 for standing in range(2, amount + 1)]
    spare, given = total - bound - (amount - 1), [1] * (amount - 1)
    while spare > 0:
        free = [i for i in range(amount - 1) if given[i] < bound]
        mass, remaining = sum([portions[i] for i in free]), spare
        for i in free:
            addition = min(bound - given[i], max(1, remaining * portions[i] // mass), spare)
            given[i] = given[i] + addition
            spare = spare - addition
    return np.array([bound] + given)


def ragged_sizes(key, number_of, total, bound, lean):
    if number_of == 2:
        one = jax.random.randint(key, (), max(1, total - bound), min(bound, total - 1) + 1)
        return jnp.stack([one, total - one])
    lengths = jnp.asarray(split_up(number_of, total, bound, lean), jnp.int32)
    pairs = (number_of - 1) // 2
    source_of, sink = lengths[1:1 + 2 * pairs:2], lengths[2:2 + 2 * pairs:2]
    margin = jnp.minimum(source_of - 1, bound - sink)
    moved = jax.random.randint(jax.random.fold_in(key, 1), (pairs,), 0, 1 << 20) % (margin + 1)
    lengths = lengths.at[1:1 + 2 * pairs:2].set(source_of - moved).at[2:2 + 2 * pairs:2].set(sink + moved)
    return lengths[jax.random.permutation(jax.random.fold_in(key, 2), number_of)]


def centred(stream_key, shape, deviation, most, pieces=(), kind=jnp.bfloat16):
    entries = deviation * jax.random.normal(stream_key, shape, jnp.float32)
    if pieces:
        entries = entries * levels(stream_key, shape, pieces, -0.22, 0.18)
    return jnp.clip(entries, -most, most).astype(kind)


def setup_inputs(seed: int = 0) -> dict:
    key_list = jax.random.split(jax.random.key(seed), 10)
    queries = draw_queries(jax.random.fold_in(key_list[9], 71), 0)
    suffix_cache = centred(key_list[1], (TOKENS, KVDIM), 0.75, 1.875, ((0, 8), (1, 4)))
    suffix_leaf = jax.vmap(lambda own: jnp.searchsorted(jnp.cumsum(ragged_sizes(own, LEAF_ROW, TOK_ROW, MOST, 2)), jnp.arange(TOK_ROW), side="right"))(jax.random.split(key_list[2], N_ROW)).reshape((N_ROW, TOK_ROW)).astype(jnp.int32)
    leaf_parent = draw_leaf_parent(jax.random.fold_in(key_list[9], 71), 0)
    root_cache = draw_root_cache(jax.random.fold_in(key_list[9], 71), 0)
    branch_cache = centred(key_list[5], (BRANCHES, BRANCH_LEN, KVDIM), 0.75, 1.875, ((0, 8), (1, 4)))
    branch_length = ragged_sizes(key_list[6], BRANCHES, 3 * BRANCHES * BRANCH_LEN // 4, BRANCH_LEN, 1).astype(jnp.int32)
    leaf_cache = centred(key_list[7], (LEAVES, LEAF_LEN, KVDIM), 0.75, 1.875, ((0, 8), (1, 4)))
    leaf_length = ragged_sizes(key_list[8], LEAVES, LEAVES * LEAF_LEN // 2, LEAF_LEN, 1).astype(jnp.int32)
    return {"queries": queries, "suffix_cache": suffix_cache, "suffix_leaf": suffix_leaf, "leaf_parent": leaf_parent, "root_cache": root_cache, "branch_cache": branch_cache, "branch_length": branch_length, "leaf_cache": leaf_cache, "leaf_length": leaf_length}


NEG = -1e+30

def finish(query_heads, key_heads, value_heads, scores, usable, row_count, equation):
    if usable is not None:
        key_mask = usable[:, None, None, :]
        scores = jnp.where(key_mask, scores, NEG)
    highest = lax.optimization_barrier(jnp.max(scores, axis=-1))
    weights = jnp.exp(scores - highest[..., None])
    if usable is not None:
        weights = jnp.where(key_mask, weights, 0.0)
    totals = lax.optimization_barrier(jnp.sum(weights, axis=-1))
    rounded = lax.optimization_barrier(weights.astype(jnp.bfloat16)).astype(jnp.float32)
    summed = jnp.einsum(equation, rounded, value_heads)
    return (highest.reshape(row_count, HEADS), totals.reshape(row_count, HEADS), summed.reshape(row_count, HEADS * HEAD_DIM))

def attend(queries, keys_values, usable):
    row_count = queries.shape[0]
    key_count = keys_values.shape[0]
    group_size = HEADS // KV_HEADS
    key_width = KV_HEADS * HEAD_DIM
    query_heads = queries.astype(jnp.float32).reshape(row_count, KV_HEADS, group_size, HEAD_DIM)
    key_heads = keys_values[:, :key_width].astype(jnp.float32).reshape(key_count, KV_HEADS, HEAD_DIM)
    value_heads = keys_values[:, key_width:].astype(jnp.float32).reshape(key_count, KV_HEADS, HEAD_DIM)
    scores = jnp.einsum('rgjd,kgd->rgjk', query_heads, key_heads) * (1.0 / math.sqrt(HEAD_DIM))
    return finish(query_heads, key_heads, value_heads, scores, usable, row_count, 'rgjk,kgd->rgjd')

def attend_each(queries, keys_values, usable):
    row_count = queries.shape[0]
    key_count = keys_values.shape[1]
    group_size = HEADS // KV_HEADS
    key_width = KV_HEADS * HEAD_DIM
    query_heads = queries.astype(jnp.float32).reshape(row_count, KV_HEADS, group_size, HEAD_DIM)
    key_heads = keys_values[:, :, :key_width].astype(jnp.float32).reshape(row_count, key_count, KV_HEADS, HEAD_DIM)
    value_heads = keys_values[:, :, key_width:].astype(jnp.float32).reshape(row_count, key_count, KV_HEADS, HEAD_DIM)
    scores = jnp.einsum('rgjd,rkgd->rgjk', query_heads, key_heads) * (1.0 / math.sqrt(HEAD_DIM))
    return finish(query_heads, key_heads, value_heads, scores, usable, row_count, 'rgjk,rkgd->rgjd')

def merge_state(earlier, others):
    highest = jnp.maximum(earlier[0], others[0])
    keep_first = jnp.exp(earlier[0] - highest)
    keep_second = jnp.exp(others[0] - highest)
    totals = earlier[1] * keep_first + others[1] * keep_second
    summed = earlier[2] * jnp.repeat(keep_first, HEAD_DIM, axis=1) + others[2] * jnp.repeat(keep_second, HEAD_DIM, axis=1)
    return (highest, totals, summed)

def reference(queries, suffix_cache, suffix_leaf, leaf_parent, root_cache, branch_cache, branch_length, leaf_cache, leaf_length):
    query_rows = queries.reshape(N_ROW, TOK_ROW, QDIM)
    suffix_rows = suffix_cache.reshape(N_ROW, TOK_ROW, KVDIM)
    row_ids = jnp.arange(N_ROW, dtype=jnp.int32)
    positions = jnp.arange(TOK_ROW, dtype=jnp.int32)
    leaf_places = jnp.arange(LEAF_LEN, dtype=jnp.int32)

    def row_local(inputs):
        row_queries, row_suffix, row_leaf, row_index = inputs
        running = attend(row_queries, root_cache, None)
        leaf_global = (row_index * LEAF_ROW + row_leaf).astype(jnp.int32)
        token_cache = leaf_cache[leaf_global]
        token_length = leaf_length[leaf_global]
        usable = leaf_places[None, :] < token_length[:, None]
        running = merge_state(running, attend_each(row_queries, token_cache, usable))
        usable = (row_leaf[:, None] == row_leaf[None, :]) & (positions[None, :] <= positions[:, None])
        running = merge_state(running, attend(row_queries, row_suffix, usable))
        return running
    local_state = lax.map(row_local, (query_rows, suffix_rows, suffix_leaf, row_ids))
    local_state = (local_state[0].reshape(TOKENS, HEADS), local_state[1].reshape(TOKENS, HEADS), local_state[2].reshape(TOKENS, QDIM))
    token_node = jnp.take_along_axis(leaf_parent, suffix_leaf, axis=1).astype(jnp.int32)
    node_hits = (token_node[:, :, None] == row_ids[None, None, :]).astype(jnp.int32)
    rank_in_node = lax.optimization_barrier(jnp.sum(node_hits * (jnp.cumsum(node_hits, axis=1) - 1), axis=2)).astype(jnp.int32)
    token_index = (row_ids[:, None] * TOK_ROW + positions[None, :]).astype(jnp.int32)
    slot_token = jnp.full((N_ROW, N_ROW, CAP), TOKENS, jnp.int32).at[token_node, row_ids[:, None], rank_in_node].set(token_index)
    padded = jnp.concatenate([queries, jnp.zeros((1, QDIM), queries.dtype)], axis=0)
    branch_places = jnp.arange(BRANCH_LEN, dtype=jnp.int32)

    def branch_part(inputs):
        node_slots, node_cache, node_length = inputs
        usable = (branch_places < node_length)[None, :]
        return attend(padded[node_slots.reshape(N_ROW * CAP)], node_cache, usable)
    branch_state = lax.map(branch_part, (slot_token, branch_cache, branch_length))
    flat_slot = (rank_in_node + row_ids[:, None] * CAP).astype(jnp.int32)
    picked = (branch_state[0][token_node, flat_slot].reshape(TOKENS, HEADS), branch_state[1][token_node, flat_slot].reshape(TOKENS, HEADS), branch_state[2][token_node, flat_slot].reshape(TOKENS, QDIM))
    highest, totals, summed = merge_state(local_state, picked)
    return (summed / jnp.repeat(totals, HEAD_DIM, axis=1)).astype(jnp.bfloat16)
```

```python
import functools
import math

import jax
import jax.numpy as jnp
from jax import lax
from jax.experimental import pallas as pl
from jax.experimental.pallas import tpu as pltpu
from jax.sharding import PartitionSpec as P

HEADS = 8
KV_HEADS = 4
HEAD_DIM = 256
LEAF_ROW = 32


NEG = -1e30


def attend(queries, keys_values, usable):
    row_count = queries.shape[0]
    key_count = keys_values.shape[0]
    group_size = HEADS // KV_HEADS
    key_width = KV_HEADS * HEAD_DIM
    query_heads = queries.reshape(row_count, KV_HEADS, group_size, HEAD_DIM)
    key_heads = keys_values[:, :key_width].reshape(key_count, KV_HEADS, HEAD_DIM)
    value_heads = keys_values[:, key_width:].reshape(key_count, KV_HEADS, HEAD_DIM)
    scores = jnp.einsum(
        "rgjd,kgd->rgjk", query_heads, key_heads, preferred_element_type=jnp.float32
    ) * (1.0 / math.sqrt(HEAD_DIM))
    if usable is not None:
        key_mask = usable[:, None, None, :]
        scores = jnp.where(key_mask, scores, NEG)
    highest = jnp.max(scores, axis=-1)
    weights = jnp.exp(scores - highest[..., None])
    if usable is not None:
        weights = jnp.where(key_mask, weights, 0.0)
    totals = jnp.sum(weights, axis=-1)
    summed = jnp.einsum(
        "rgjk,kgd->rgjd",
        weights.astype(jnp.bfloat16),
        value_heads,
        preferred_element_type=jnp.float32,
    )
    return (
        highest.reshape(row_count, HEADS),
        totals.reshape(row_count, HEADS),
        summed.reshape(row_count, HEADS * HEAD_DIM),
    )


def merge_state(earlier, others):
    highest = jnp.maximum(earlier[0], others[0])
    keep_first = jnp.exp(earlier[0] - highest)
    keep_second = jnp.exp(others[0] - highest)
    totals = earlier[1] * keep_first + others[1] * keep_second
    summed = earlier[2] * jnp.repeat(keep_first, HEAD_DIM, axis=1) + others[2] * jnp.repeat(
        keep_second, HEAD_DIM, axis=1
    )
    return (highest, totals, summed)


def slice_heads(values, col_index, feature_width):
    per_slice = max(1, feature_width // HEAD_DIM)
    first_head = col_index * feature_width // HEAD_DIM
    chosen = lax.dynamic_slice_in_dim(values, first_head, per_slice, values.ndim - 1)
    return jnp.repeat(chosen, feature_width // per_slice, axis=values.ndim - 1)


def combine_columns(running):
    highest, totals, summed = running
    overall = lax.pmax(highest, "col")
    factors = jnp.exp(highest - overall)
    slice_sum = lax.psum_scatter(
        summed * jnp.repeat(factors, HEAD_DIM, axis=1), "col", scatter_dimension=1, tiled=True
    )
    overall_total = lax.psum(totals * factors, "col")
    return (overall, overall_total, slice_sum)


def on_device(
    queries,
    suffix_cache,
    suffix_leaf,
    leaf_parent,
    root_cache,
    branch_cache,
    branch_length,
    leaf_cache,
    leaf_length,
):
    col_count = lax.axis_size("col")
    row_count = lax.axis_size("row")
    col_index = lax.axis_index("col")
    full_queries, full_suffix = (
        lax.all_gather(queries, "col", axis=1, tiled=True),
        lax.all_gather(suffix_cache, "col", axis=1, tiled=True),
    )
    token_count = full_queries.shape[0]
    query_width = full_queries.shape[1]
    feature_width = queries.shape[1]
    leaf_local = suffix_leaf[0]
    positions = jnp.arange(token_count, dtype=jnp.int32)
    blank_state = (
        jnp.full((token_count, HEADS), NEG, jnp.float32),
        jnp.zeros((token_count, HEADS), jnp.float32),
        jnp.zeros((token_count, query_width), jnp.float32),
    )
    running = merge_state(
        blank_state,
        attend(full_queries, lax.all_gather(root_cache, "row", axis=0, tiled=True), None),
    )
    leaf_width = leaf_cache.shape[1]
    leaf_keys = leaf_cache.reshape(LEAF_ROW * leaf_width, leaf_cache.shape[2])
    key_slot = jnp.arange(LEAF_ROW * leaf_width, dtype=jnp.int32)
    key_leaf = key_slot // leaf_width
    key_place = col_index * leaf_width + key_slot % leaf_width
    leaf_ids = jnp.arange(LEAF_ROW, dtype=jnp.int32)
    key_live = jnp.any(
        (key_leaf[None, :] == leaf_ids[:, None]) & (key_place[None, :] < leaf_length[:, None]),
        axis=0,
    )
    usable = (leaf_local[:, None] == key_leaf[None, :]) & key_live[None, :]
    running = merge_state(running, attend(full_queries, leaf_keys, usable))
    suffix_width = token_count // col_count
    suffix_start = col_index * suffix_width
    suffix_keys = lax.dynamic_slice_in_dim(full_suffix, suffix_start, suffix_width, 0)
    suffix_owner = lax.dynamic_slice_in_dim(leaf_local, suffix_start, suffix_width, 0)
    suffix_place = suffix_start + jnp.arange(suffix_width, dtype=jnp.int32)
    usable = (leaf_local[:, None] == suffix_owner[None, :]) & (
        suffix_place[None, :] <= positions[:, None]
    )
    running = merge_state(running, attend(full_queries, suffix_keys, usable))
    parents = leaf_parent[0]
    token_node = jnp.sum(
        jnp.where(leaf_local[:, None] == leaf_ids[None, :], parents[None, :], 0), axis=1
    )
    node_ids = jnp.arange(row_count, dtype=jnp.int32)
    node_hits = (token_node[:, None] == node_ids[None, :]).astype(jnp.int32)
    rank_in_node = jnp.sum(node_hits * (jnp.cumsum(node_hits, axis=0) - 1), axis=1)
    capacity = token_count // 16 * (LEAF_ROW // row_count)
    slot_index = token_node * capacity + rank_in_node
    slot_token = (
        jnp.full((row_count * capacity,), token_count, jnp.int32).at[slot_index].set(positions)
    )
    padded = jnp.concatenate(
        [full_queries, jnp.zeros((1, query_width), full_queries.dtype)], axis=0
    )
    outgoing = padded[slot_token].reshape(row_count, capacity, query_width)
    branch_keys = branch_cache[0]
    branch_width = branch_keys.shape[0]
    branch_place = col_index * branch_width + jnp.arange(branch_width, dtype=jnp.int32)
    branch_usable = (branch_place < branch_length[0])[None, :]
    arrived = lax.all_to_all(outgoing, "row", split_axis=0, concat_axis=0, tiled=True)
    sources = arrived.shape[0]
    item_count = arrived.shape[1]
    flat_queries = arrived.reshape(sources * item_count, arrived.shape[2])
    highest, totals, summed = attend(flat_queries, branch_keys, branch_usable)
    returned = (
        lax.all_to_all(
            summed.reshape(sources, item_count, query_width),
            "row",
            split_axis=0,
            concat_axis=0,
            tiled=True,
        ),
        lax.all_to_all(
            highest.reshape(sources, item_count, HEADS),
            "row",
            split_axis=0,
            concat_axis=0,
            tiled=True,
        ),
        lax.all_to_all(
            totals.reshape(sources, item_count, HEADS),
            "row",
            split_axis=0,
            concat_axis=0,
            tiled=True,
        ),
    )
    back_sums = returned[0].reshape(row_count * capacity, returned[0].shape[2])[slot_index]
    back_peaks = returned[1].reshape(row_count * capacity, HEADS)[slot_index]
    back_totals = returned[2].reshape(row_count * capacity, HEADS)[slot_index]
    running = merge_state(running, (back_peaks, back_totals, back_sums))
    highest, totals, summed = combine_columns(running)
    output = summed / slice_heads(totals, col_index, feature_width)
    return output.astype(jnp.bfloat16)


LOW = -1e29
LOG2_SCALE = 1.0 / (math.sqrt(HEAD_DIM) * math.log(2.0))
KEY_WIDTH = KV_HEADS * HEAD_DIM
PAIR = HEADS // KV_HEADS * HEAD_DIM
KEY_STEP = 1024
NT = (((1,), (1,)), ((), ()))
NN = (((1,), (0,)), ((), ()))


def dot(a, b, dims=NN, precision=None):
    return lax.dot_general(a, b, dims, precision=precision, preferred_element_type=jnp.float32)


def state_of(query_rows, keys, values, mask):
    scores = dot(query_rows, keys, NT) * LOG2_SCALE
    if mask is not None:
        scores = jnp.where(mask, scores, NEG)
    highest = jnp.maximum(jnp.max(scores, axis=1, keepdims=True), LOW)
    weights = jnp.exp2(scores - highest)
    totals = jnp.sum(weights, axis=1, keepdims=True)
    return highest, totals, dot(weights.astype(jnp.bfloat16), values)


def join(first, second):
    highest = jnp.maximum(first[0], second[0])
    a, b = jnp.exp2(first[0] - highest), jnp.exp2(second[0] - highest)
    return highest, first[1] * a + second[1] * b, first[2] * a + second[2] * b


def stacked(pair):
    return jnp.concatenate([pair[:, :HEAD_DIM], pair[:, HEAD_DIM:]], axis=0)


def fused_kernel(
    n_row, n_col, cap,
    q_ref, suf_ref, leaf_of_ref, parent_ref, leaf_len_ref, branch_len_ref, root_ref, branch_ref, leaf_ref,
    out_ref,
    qg, sbuf, rootb, leafv, branchv, sendq, brq, bro, brs, ret, rets, lm, ll, lo, fo, fs, fin, fins,
    load_sem, q_s, q_r, suf_s, suf_r, root_s, root_r, fwd_s, fwd_r, bq_s, bq_r, bo_s, bo_r, bs_s, bs_r,
    f_s, f_r, fs_s, fs_r,
):
    row, col = lax.axis_index("row"), lax.axis_index("col")
    tokens = q_ref.shape[0]
    slots = n_row * cap
    branch_keys, leaf_keys = branchv.shape[0], leafv.shape[0]
    leaf_width = leaf_keys // LEAF_ROW

    def copy_to(src, dst, s, r, **where):
        return pltpu.make_async_remote_copy(
            src_ref=src, dst_ref=dst, send_sem=s, recv_sem=r, device_id=where,
            device_id_type=pl.DeviceIdType.MESH,
        )

    loads = []
    for i, (src, dst) in enumerate(((leaf_ref, leafv), (branch_ref, branchv))):
        step = dst.shape[0] // 2
        for j in range(2):
            part = pl.ds(j * step, step)
            loads.append(pltpu.make_async_copy(src.at[part], dst.at[part], load_sem.at[2 * i + j]))
    for load in loads:
        load.start()

    barrier = pltpu.get_barrier_semaphore()
    for k in range(1, n_row):
        pl.semaphore_signal(barrier, inc=1, device_id={"row": (row + k) % n_row},
                            device_id_type=pl.DeviceIdType.MESH)
    for k in range(1, n_col):
        pl.semaphore_signal(barrier, inc=1, device_id={"col": (col + k) % n_col},
                            device_id_type=pl.DeviceIdType.MESH)
    pl.semaphore_wait(barrier, n_row + n_col - 2)

    sent = []

    def send(copy):
        copy.start()
        sent.append(copy)
        return copy

    q_copies = [
        send(copy_to(q_ref, qg.at[col], q_s.at[k], q_r.at[k], col=(col + k) % n_col))
        for k in range(1, n_col)
    ]
    mate = row + 1 - 2 * (row % 2)

    def root_copy(i, peer):
        return copy_to(root_ref, rootb.at[row], root_s.at[i], root_r.at[i], row=peer)

    def flip(k):
        bit = 2 ** k
        return row + bit - 2 * bit * ((row // bit) % 2)

    flips = (flip(1), flip(2), n_row - 2 + 2 * (row % 2) - row)
    root_copies = [send(root_copy(0, mate)), send(root_copy(1, flips[0])), send(root_copy(2, flips[1]))]
    first = 2 * (col % 2)
    for h in range(2):
        @pl.when(first + h != col)
        def _():
            copy_to(suf_ref.at[:, pl.ds(h * HEAD_DIM, HEAD_DIM)], sbuf.at[col // 2], suf_s.at[h],
                    suf_r.at[col // 2], col=first + h).start()

        @pl.when(first + h == col)
        def _():
            sbuf[col // 2] = suf_ref[:, h * HEAD_DIM:(h + 1) * HEAD_DIM]
    qg[col] = q_ref[...]
    rootb[row] = root_ref[...]

    def eye(n):
        return lax.broadcasted_iota(jnp.int32, (n, n), 0) == lax.broadcasted_iota(jnp.int32, (n, n), 1)

    def to_column(values):
        return jnp.sum(jnp.where(eye(values.shape[1]), values, 0.0), axis=1, keepdims=True)

    def to_row(values):
        return jnp.sum(jnp.where(eye(values.shape[0]), values, 0.0), axis=0, keepdims=True)

    leaf_row = leaf_of_ref[...].astype(jnp.float32)
    leaf_col = to_column(leaf_row)
    parent_row = parent_ref[...].astype(jnp.float32)
    leaf_iota = lax.broadcasted_iota(jnp.int32, (tokens, LEAF_ROW), 1).astype(jnp.float32)
    node_col = jnp.sum(jnp.where(leaf_col == leaf_iota, parent_row, 0.0), axis=1, keepdims=True)
    node_row = to_row(node_col)
    above = lax.broadcasted_iota(jnp.int32, (tokens, tokens), 0)
    along = lax.broadcasted_iota(jnp.int32, (tokens, tokens), 1)
    earlier = jnp.where((node_col == node_row) & (along < above), 1.0, 0.0)
    slot_col = node_col * cap + jnp.sum(earlier, axis=1, keepdims=True)
    slot_row = to_row(slot_col)
    spread = jnp.where(
        lax.broadcasted_iota(jnp.int32, (slots, tokens), 0).astype(jnp.float32) == slot_row, 1.0, 0.0
    ).astype(jnp.bfloat16)
    collect = jnp.where(
        lax.broadcasted_iota(jnp.int32, (tokens, slots), 1).astype(jnp.float32) == slot_col, 1.0, 0.0
    )
    len_col = to_column(leaf_len_ref[...].astype(jnp.float32))
    key_at = lax.broadcasted_iota(jnp.int32, (1, leaf_keys), 1)
    key_leaf = (key_at // leaf_width).astype(jnp.float32)
    key_place = (col * leaf_width + key_at % leaf_width).astype(jnp.float32)
    rows32 = lax.broadcasted_iota(jnp.int32, (LEAF_ROW, leaf_keys), 0).astype(jnp.float32)
    key_len = jnp.sum(jnp.where(rows32 == key_leaf, len_col, 0.0), axis=0, keepdims=True)
    key_leaf = jnp.where(key_place < key_len, key_leaf, -1.0)
    leaf_col2 = jnp.concatenate([leaf_col, leaf_col], axis=0)

    for copy in q_copies:
        copy.wait_recv()
    for g in range(n_col):
        gathered = dot(spread, qg[g]).astype(jnp.bfloat16)
        sendq[:, :, g * PAIR:(g + 1) * PAIR] = gathered.reshape(n_row, cap, PAIR)
    bq_copies = []
    for k in range(1, n_row):
        peer = (row + k) % n_row
        bq_copies.append(send(copy_to(sendq.at[peer], brq.at[row], bq_s.at[k], bq_r.at[k], row=peer)))
    root_copies.append(send(root_copy(3, flips[2])))
    brq[row] = sendq[row]

    loads[0].wait()
    loads[1].wait()

    def leaf_level(g, carry):
        rows = stacked(qg[g])
        states = []
        for at in range(0, leaf_keys, KEY_STEP):
            keys = leafv[at:at + KEY_STEP, pl.ds(pl.multiple_of(g * HEAD_DIM, HEAD_DIM), HEAD_DIM)]
            values = leafv[
                at:at + KEY_STEP, pl.ds(pl.multiple_of(KEY_WIDTH + g * HEAD_DIM, HEAD_DIM), HEAD_DIM)
            ]
            states.append(state_of(rows, keys, values, leaf_col2 == key_leaf[:, at:at + KEY_STEP]))
        lm[g], ll[g], lo[g] = join(*states)
        return carry

    lax.fori_loop(0, KV_HEADS, leaf_level, 0)

    fwd_copies = []
    for i in range(2):
        root_copies[1 + i].wait_recv()
        fwd_copies.append(send(copy_to(rootb.at[flips[i]], rootb.at[flips[i]], fwd_s.at[i],
                                       fwd_r.at[i], row=mate)))

    for copy in bq_copies:
        copy.wait_recv()
    loads[2].wait()
    loads[3].wait()
    brs[...] = jnp.zeros_like(brs)

    def branch_out(g, k):
        peer = (row + k) % n_row
        return copy_to(bro.at[g, peer], ret.at[g, row], bo_s.at[g, k], bo_r.at[g, k], row=peer)

    def branch_level(g, carry):
        rows = stacked(brq[:, :, pl.ds(pl.multiple_of(g * PAIR, PAIR), PAIR)].reshape(slots, PAIR))
        states = []
        for at in range(0, branch_keys, KEY_STEP):
            keys = branchv[at:at + KEY_STEP, pl.ds(pl.multiple_of(g * HEAD_DIM, HEAD_DIM), HEAD_DIM)]
            values = branchv[
                at:at + KEY_STEP, pl.ds(pl.multiple_of(KEY_WIDTH + g * HEAD_DIM, HEAD_DIM), HEAD_DIM)
            ]
            place = col * branch_keys + at + lax.broadcasted_iota(jnp.int32, (1, KEY_STEP), 1)
            states.append(state_of(rows, keys, values, place < branch_len_ref[...]))
        highest, totals, summed = join(*states)
        lane = lax.broadcasted_iota(jnp.int32, (slots, 128), 1)
        stat = brs[...].reshape(slots, 128)
        for j in range(2):
            stat = jnp.where(lane == 4 * g + j, highest[j * slots:(j + 1) * slots], stat)
            stat = jnp.where(lane == 4 * g + 2 + j, totals[j * slots:(j + 1) * slots], stat)
        brs[...] = stat.reshape(n_row, cap, 128)
        summed = jnp.concatenate([summed[:slots], summed[slots:]], axis=1).astype(jnp.bfloat16)
        bro[g] = summed.reshape(n_row, cap, PAIR)
        for k in range(1, n_row):
            branch_out(g, k).start()
        return carry

    lax.fori_loop(0, KV_HEADS, branch_level, 0)
    bs_copies = []
    for k in range(1, n_row):
        peer = (row + k) % n_row
        bs_copies.append(send(copy_to(brs.at[peer], rets.at[row], bs_s.at[k], bs_r.at[k], row=peer)))
    rets[row] = brs[row]
    for g in range(KV_HEADS):
        ret[g, row] = bro[g, row]

    root_copies[3].wait_recv()
    fwd_copies.append(send(copy_to(rootb.at[flips[2]], rootb.at[flips[2]], fwd_s.at[2], fwd_r.at[2],
                                   row=mate)))
    root_copies[0].wait_recv()
    for copy in fwd_copies:
        copy.wait_recv()

    def root_level(g, carry):
        rows = stacked(qg[g])
        keys = rootb[:, :, pl.ds(pl.multiple_of(g * HEAD_DIM, HEAD_DIM), HEAD_DIM)]
        values = rootb[:, :, pl.ds(pl.multiple_of(KEY_WIDTH + g * HEAD_DIM, HEAD_DIM), HEAD_DIM)]
        keys, values = keys.reshape(-1, HEAD_DIM), values.reshape(-1, HEAD_DIM)
        lm[g], ll[g], lo[g] = join((lm[g], ll[g], lo[g]), state_of(rows, keys, values, None))
        return carry

    lax.fori_loop(0, KV_HEADS, root_level, 0)

    for copy in bs_copies:
        copy.wait_recv()
    stats = dot(collect, rets[...].reshape(slots, 128), precision=lax.Precision.HIGHEST)
    collect16 = collect.astype(jnp.bfloat16)
    lane = lax.broadcasted_iota(jnp.int32, (tokens, 128), 1)

    def pick(index):
        return jnp.sum(jnp.where(lane == index, stats, 0.0), axis=1, keepdims=True)

    def final_copies(g):
        return (
            copy_to(fo.at[g], fin.at[col], f_s.at[g], f_r.at[col], col=g),
            copy_to(fs.at[g], fins.at[col], fs_s.at[g], fs_r.at[col], col=g),
        )

    for g in range(KV_HEADS):
        for k in range(1, n_row):
            branch_out(g, k).wait_recv()
        back = dot(collect16, ret[g].reshape(slots, PAIR))
        summed, lines = [], []
        for j in range(2):
            part = slice(j * tokens, (j + 1) * tokens)
            state = join(
                (lm[g, part], ll[g, part], lo[g, part]),
                (pick(4 * g + j), pick(4 * g + 2 + j), back[:, j * HEAD_DIM:(j + 1) * HEAD_DIM]),
            )
            summed.append(state[2])
            lines += [to_row(state[0]), to_row(state[1])]
        fo[g] = jnp.concatenate(summed, axis=1).astype(jnp.bfloat16)
        fs[g] = jnp.concatenate(lines + lines, axis=0)

        @pl.when(col != g)
        def _():
            for copy in final_copies(g):
                copy.start()

    for i, local in ((0, 0), (1, n_col - 1)):
        @pl.when(col != local)
        def _():
            copy_to(suf_ref.at[:, pl.ds(0, HEAD_DIM)], sbuf.at[i], suf_s.at[0], suf_r.at[i],
                    col=(col + 1) % n_col).wait_recv()
    mask = (leaf_col2 == leaf_row) & (
        lax.broadcasted_iota(jnp.int32, (2 * tokens, tokens), 1)
        <= lax.broadcasted_iota(jnp.int32, (2 * tokens, tokens), 0) % tokens
    )
    state = state_of(stacked(q_ref[...]), sbuf[0], sbuf[1], mask)
    fin[col] = fo[col]
    fins[col] = fs[col]
    for g in range(n_col):
        @pl.when(col != g)
        def _():
            peer = g
            copy_to(fo.at[g], fin.at[peer], f_s.at[g], f_r.at[peer], col=g).wait_recv()
            copy_to(fs.at[g], fins.at[peer], fs_s.at[g], fs_r.at[peer], col=g).wait_recv()
    for j in range(2):
        part = slice(j * tokens, (j + 1) * tokens)
        mine = tuple(entry[part] for entry in state)
        for g in range(n_col):
            lines = fins[g]
            mine = join(mine, (
                to_column(lines[2 * j:2 * j + 1]), to_column(lines[2 * j + 1:2 * j + 2]),
                fin[g, :, j * HEAD_DIM:(j + 1) * HEAD_DIM].astype(jnp.float32),
            ))
        out_ref[:, j * HEAD_DIM:(j + 1) * HEAD_DIM] = (mine[2] / mine[1]).astype(out_ref.dtype)

    for copy in sent:
        copy.wait_send()
    for h in range(2):
        @pl.when(first + h != col)
        def _():
            copy_to(suf_ref.at[:, pl.ds(h * HEAD_DIM, HEAD_DIM)], sbuf.at[col // 2], suf_s.at[h],
                    suf_r.at[col // 2], col=first + h).wait_send()
    for g in range(KV_HEADS):
        for k in range(1, n_row):
            branch_out(g, k).wait_send()

        @pl.when(col != g)
        def _():
            for copy in final_copies(g):
                copy.wait_send()


def on_device_fused(
    queries, suffix_cache, suffix_leaf, leaf_parent, root_cache, branch_cache, branch_length, leaf_cache,
    leaf_length,
):
    n_row, n_col = lax.axis_size("row"), lax.axis_size("col")
    tokens = queries.shape[0]
    cap = tokens // 16 * (LEAF_ROW // n_row)
    slots = n_row * cap
    width = branch_cache.shape[2]
    branch = branch_cache.reshape(-1, width)
    leaf = leaf_cache.reshape(-1, width)
    bf16, f32 = jnp.bfloat16, jnp.float32
    dma = pltpu.SemaphoreType.DMA
    vmem = pltpu.VMEM
    scratch = [
        vmem((n_col, tokens, PAIR), bf16),
        vmem((2, tokens, HEAD_DIM), bf16),
        vmem((n_row,) + root_cache.shape, bf16),
        vmem(leaf.shape, bf16),
        vmem(branch.shape, bf16),
        vmem((n_row, cap, width), bf16),
        vmem((n_row, cap, width), bf16),
        vmem((KV_HEADS, n_row, cap, PAIR), bf16),
        vmem((n_row, cap, 128), f32),
        vmem((KV_HEADS, n_row, cap, PAIR), bf16),
        vmem((n_row, cap, 128), f32),
        vmem((KV_HEADS, 2 * tokens, 1), f32),
        vmem((KV_HEADS, 2 * tokens, 1), f32),
        vmem((KV_HEADS, 2 * tokens, HEAD_DIM), f32),
        vmem((KV_HEADS, tokens, PAIR), bf16),
        vmem((KV_HEADS, 8, tokens), f32),
        vmem((n_col, tokens, PAIR), bf16),
        vmem((n_col, 8, tokens), f32),
        dma((4,)),
        dma((n_col,)), dma((n_col,)),
        dma((2,)), dma((2,)),
        dma((4,)), dma((4,)),
        dma((3,)), dma((3,)),
        dma((n_row,)), dma((n_row,)),
        dma((KV_HEADS, n_row)), dma((KV_HEADS, n_row)),
        dma((n_row,)), dma((n_row,)),
        dma((n_col,)), dma((n_col,)),
        dma((n_col,)), dma((n_col,)),
    ]
    in_vmem = pl.BlockSpec(memory_space=pltpu.VMEM)
    anywhere = pl.BlockSpec(memory_space=pl.ANY)
    return pl.pallas_call(
        functools.partial(fused_kernel, n_row, n_col, cap),
        out_shape=jax.ShapeDtypeStruct(queries.shape, queries.dtype),
        in_specs=[in_vmem] * 7 + [anywhere] * 2,
        out_specs=in_vmem,
        scratch_shapes=scratch,
        compiler_params=pltpu.CompilerParams(
            collective_id=0, has_side_effects=True, vmem_limit_bytes=56 * 2**20
        ),
    )(
        queries, suffix_cache, suffix_leaf, leaf_parent, leaf_length.reshape(1, -1),
        branch_length.reshape(1, 1), root_cache, branch, leaf,
    )


def solution(mesh):
    in_specs = (
        P("row", "col"),
        P("row", "col"),
        P("row", None),
        P("row", None),
        P(("row", "col"), None),
        P("row", "col", None),
        P("row"),
        P("row", "col", None),
        P("row"),
    )
    out_specs = P("row", "col")
    sizes = dict(mesh.shape)
    body = on_device_fused if (sizes["row"], sizes["col"]) == (8, 4) else on_device
    return jax.shard_map(
        body, mesh=mesh, in_specs=in_specs, out_specs=out_specs, check_vma=False
    )
```

```python
import functools
import math

import jax
import jax.numpy as jnp
from jax import lax
from jax.experimental import pallas as pl
from jax.experimental.pallas import tpu as pltpu
from jax.sharding import PartitionSpec as P

HEADS = 8
KV_HEADS = 4
HEAD_DIM = 256
LEAF_ROW = 32


NEG = -1e30


def attend(queries, keys_values, usable):
    row_count = queries.shape[0]
    key_count = keys_values.shape[0]
    group_size = HEADS // KV_HEADS
    key_width = KV_HEADS * HEAD_DIM
    query_heads = queries.reshape(row_count, KV_HEADS, group_size, HEAD_DIM)
    key_heads = keys_values[:, :key_width].reshape(key_count, KV_HEADS, HEAD_DIM)
    value_heads = keys_values[:, key_width:].reshape(key_count, KV_HEADS, HEAD_DIM)
    scores = jnp.einsum(
        "rgjd,kgd->rgjk", query_heads, key_heads, preferred_element_type=jnp.float32
    ) * (1.0 / math.sqrt(HEAD_DIM))
    if usable is not None:
        key_mask = usable[:, None, None, :]
        scores = jnp.where(key_mask, scores, NEG)
    highest = jnp.max(scores, axis=-1)
    weights = jnp.exp(scores - highest[..., None])
    if usable is not None:
        weights = jnp.where(key_mask, weights, 0.0)
    totals = jnp.sum(weights, axis=-1)
    summed = jnp.einsum(
        "rgjk,kgd->rgjd",
        weights.astype(jnp.bfloat16),
        value_heads,
        preferred_element_type=jnp.float32,
    )
    return (
        highest.reshape(row_count, HEADS),
        totals.reshape(row_count, HEADS),
        summed.reshape(row_count, HEADS * HEAD_DIM),
    )


def merge_state(earlier, others):
    highest = jnp.maximum(earlier[0], others[0])
    keep_first = jnp.exp(earlier[0] - highest)
    keep_second = jnp.exp(others[0] - highest)
    totals = earlier[1] * keep_first + others[1] * keep_second
    summed = earlier[2] * jnp.repeat(keep_first, HEAD_DIM, axis=1) + others[2] * jnp.repeat(
        keep_second, HEAD_DIM, axis=1
    )
    return (highest, totals, summed)


def slice_heads(values, col_index, feature_width):
    per_slice = max(1, feature_width // HEAD_DIM)
    first_head = col_index * feature_width // HEAD_DIM
    chosen = lax.dynamic_slice_in_dim(values, first_head, per_slice, values.ndim - 1)
    return jnp.repeat(chosen, feature_width // per_slice, axis=values.ndim - 1)


def combine_columns(running):
    highest, totals, summed = running
    overall = lax.pmax(highest, "col")
    factors = jnp.exp(highest - overall)
    slice_sum = lax.psum_scatter(
        summed * jnp.repeat(factors, HEAD_DIM, axis=1), "col", scatter_dimension=1, tiled=True
    )
    overall_total = lax.psum(totals * factors, "col")
    return (overall, overall_total, slice_sum)


def on_device(
    queries,
    suffix_cache,
    suffix_leaf,
    leaf_parent,
    root_cache,
    branch_cache,
    branch_length,
    leaf_cache,
    leaf_length,
):
    col_count = lax.axis_size("col")
    row_count = lax.axis_size("row")
    col_index = lax.axis_index("col")
    full_queries, full_suffix = (
        lax.all_gather(queries, "col", axis=1, tiled=True),
        lax.all_gather(suffix_cache, "col", axis=1, tiled=True),
    )
    token_count = full_queries.shape[0]
    query_width = full_queries.shape[1]
    feature_width = queries.shape[1]
    leaf_local = suffix_leaf[0]
    positions = jnp.arange(token_count, dtype=jnp.int32)
    blank_state = (
        jnp.full((token_count, HEADS), NEG, jnp.float32),
        jnp.zeros((token_count, HEADS), jnp.float32),
        jnp.zeros((token_count, query_width), jnp.float32),
    )
    running = merge_state(
        blank_state,
        attend(full_queries, lax.all_gather(root_cache, "row", axis=0, tiled=True), None),
    )
    leaf_width = leaf_cache.shape[1]
    leaf_keys = leaf_cache.reshape(LEAF_ROW * leaf_width, leaf_cache.shape[2])
    key_slot = jnp.arange(LEAF_ROW * leaf_width, dtype=jnp.int32)
    key_leaf = key_slot // leaf_width
    key_place = col_index * leaf_width + key_slot % leaf_width
    leaf_ids = jnp.arange(LEAF_ROW, dtype=jnp.int32)
    key_live = jnp.any(
        (key_leaf[None, :] == leaf_ids[:, None]) & (key_place[None, :] < leaf_length[:, None]),
        axis=0,
    )
    usable = (leaf_local[:, None] == key_leaf[None, :]) & key_live[None, :]
    running = merge_state(running, attend(full_queries, leaf_keys, usable))
    suffix_width = token_count // col_count
    suffix_start = col_index * suffix_width
    suffix_keys = lax.dynamic_slice_in_dim(full_suffix, suffix_start, suffix_width, 0)
    suffix_owner = lax.dynamic_slice_in_dim(leaf_local, suffix_start, suffix_width, 0)
    suffix_place = suffix_start + jnp.arange(suffix_width, dtype=jnp.int32)
    usable = (leaf_local[:, None] == suffix_owner[None, :]) & (
        suffix_place[None, :] <= positions[:, None]
    )
    running = merge_state(running, attend(full_queries, suffix_keys, usable))
    parents = leaf_parent[0]
    token_node = jnp.sum(
        jnp.where(leaf_local[:, None] == leaf_ids[None, :], parents[None, :], 0), axis=1
    )
    node_ids = jnp.arange(row_count, dtype=jnp.int32)
    node_hits = (token_node[:, None] == node_ids[None, :]).astype(jnp.int32)
    rank_in_node = jnp.sum(node_hits * (jnp.cumsum(node_hits, axis=0) - 1), axis=1)
    capacity = token_count // 16 * (LEAF_ROW // row_count)
    slot_index = token_node * capacity + rank_in_node
    slot_token = (
        jnp.full((row_count * capacity,), token_count, jnp.int32).at[slot_index].set(positions)
    )
    padded = jnp.concatenate(
        [full_queries, jnp.zeros((1, query_width), full_queries.dtype)], axis=0
    )
    outgoing = padded[slot_token].reshape(row_count, capacity, query_width)
    branch_keys = branch_cache[0]
    branch_width = branch_keys.shape[0]
    branch_place = col_index * branch_width + jnp.arange(branch_width, dtype=jnp.int32)
    branch_usable = (branch_place < branch_length[0])[None, :]
    arrived = lax.all_to_all(outgoing, "row", split_axis=0, concat_axis=0, tiled=True)
    sources = arrived.shape[0]
    item_count = arrived.shape[1]
    flat_queries = arrived.reshape(sources * item_count, arrived.shape[2])
    highest, totals, summed = attend(flat_queries, branch_keys, branch_usable)
    returned = (
        lax.all_to_all(
            summed.reshape(sources, item_count, query_width),
            "row",
            split_axis=0,
            concat_axis=0,
            tiled=True,
        ),
        lax.all_to_all(
            highest.reshape(sources, item_count, HEADS),
            "row",
            split_axis=0,
            concat_axis=0,
            tiled=True,
        ),
        lax.all_to_all(
            totals.reshape(sources, item_count, HEADS),
            "row",
            split_axis=0,
            concat_axis=0,
            tiled=True,
        ),
    )
    back_sums = returned[0].reshape(row_count * capacity, returned[0].shape[2])[slot_index]
    back_peaks = returned[1].reshape(row_count * capacity, HEADS)[slot_index]
    back_totals = returned[2].reshape(row_count * capacity, HEADS)[slot_index]
    running = merge_state(running, (back_peaks, back_totals, back_sums))
    highest, totals, summed = combine_columns(running)
    output = summed / slice_heads(totals, col_index, feature_width)
    return output.astype(jnp.bfloat16)


LOW = -1e29
LOG2_SCALE = 1.0 / (math.sqrt(HEAD_DIM) * math.log(2.0))
KEY_WIDTH = KV_HEADS * HEAD_DIM
PAIR = HEADS // KV_HEADS * HEAD_DIM
KEY_STEP = 1024
NT = (((1,), (1,)), ((), ()))
NN = (((1,), (0,)), ((), ()))


def dot(a, b, dims=NN, precision=None):
    return lax.dot_general(a, b, dims, precision=precision, preferred_element_type=jnp.float32)


def state_of(query_rows, keys, values, mask):
    scores = dot(query_rows, keys, NT) * LOG2_SCALE
    if mask is not None:
        scores = jnp.where(mask, scores, NEG)
    highest = jnp.maximum(jnp.max(scores, axis=1, keepdims=True), LOW)
    weights = jnp.exp2(scores - highest)
    totals = jnp.sum(weights, axis=1, keepdims=True)
    return highest, totals, dot(weights.astype(jnp.bfloat16), values)


def join(first, second):
    highest = jnp.maximum(first[0], second[0])
    a, b = jnp.exp2(first[0] - highest), jnp.exp2(second[0] - highest)
    return highest, first[1] * a + second[1] * b, first[2] * a + second[2] * b


def stacked(pair):
    return jnp.concatenate([pair[:, :HEAD_DIM], pair[:, HEAD_DIM:]], axis=0)


def fused_kernel(
    n_row, n_col, cap,
    q_ref, suf_ref, leaf_of_ref, parent_ref, leaf_len_ref, branch_len_ref, root_ref, branch_ref, leaf_ref,
    out_ref,
    qg, sbuf, rootb, leafv, branchv, sendq, brq, bro, bst, ret, rst, lm, ll, lo, fo, fs, fin, fins,
    load_sem, q_s, q_r, suf_s, suf_r, root_s, root_r, fwd_s, fwd_r, bq_s, bq_r, bo_s, bo_r, bs_s, bs_r,
    f_s, f_r, fs_s, fs_r,
):
    row, col = lax.axis_index("row"), lax.axis_index("col")
    tokens = q_ref.shape[0]
    slots = n_row * cap
    branch_keys, leaf_keys = branchv.shape[0], leafv.shape[0]
    leaf_width = leaf_keys // LEAF_ROW

    def copy_to(src, dst, s, r, **where):
        return pltpu.make_async_remote_copy(
            src_ref=src, dst_ref=dst, send_sem=s, recv_sem=r, device_id=where,
            device_id_type=pl.DeviceIdType.MESH,
        )

    def group(i):
        return (col + i) % 2 + 2 * ((col // 2 + i // 2) % 2)

    def head_lanes(i):
        return pl.ds(pl.multiple_of(group(i) * HEAD_DIM, HEAD_DIM), HEAD_DIM)

    def value_lanes(i):
        return pl.ds(pl.multiple_of(KEY_WIDTH + group(i) * HEAD_DIM, HEAD_DIM), HEAD_DIM)

    loads = []
    for i, (src, dst) in enumerate(((leaf_ref, leafv), (branch_ref, branchv))):
        step = dst.shape[0] // 2
        for j in range(2):
            part = pl.ds(j * step, step)
            loads.append(pltpu.make_async_copy(src.at[part], dst.at[part], load_sem.at[2 * i + j]))
    for load in loads:
        load.start()

    barrier = pltpu.get_barrier_semaphore()
    for k in range(1, n_row):
        pl.semaphore_signal(barrier, inc=1, device_id={"row": (row + k) % n_row},
                            device_id_type=pl.DeviceIdType.MESH)
    for k in range(1, n_col):
        pl.semaphore_signal(barrier, inc=1, device_id={"col": (col + k) % n_col},
                            device_id_type=pl.DeviceIdType.MESH)

    def eye(n):
        return lax.broadcasted_iota(jnp.int32, (n, n), 0) == lax.broadcasted_iota(jnp.int32, (n, n), 1)

    def to_column(values):
        return jnp.sum(jnp.where(eye(values.shape[1]), values, 0.0), axis=1, keepdims=True)

    def to_row(values):
        return jnp.sum(jnp.where(eye(values.shape[0]), values, 0.0), axis=0, keepdims=True)

    leaf_row = leaf_of_ref[...].astype(jnp.float32)
    leaf_col = to_column(leaf_row)
    parent_row = parent_ref[...].astype(jnp.float32)
    leaf_iota = lax.broadcasted_iota(jnp.int32, (tokens, LEAF_ROW), 1).astype(jnp.float32)
    node_col = jnp.sum(jnp.where(leaf_col == leaf_iota, parent_row, 0.0), axis=1, keepdims=True)
    node_row = to_row(node_col)
    above = lax.broadcasted_iota(jnp.int32, (tokens, tokens), 0)
    along = lax.broadcasted_iota(jnp.int32, (tokens, tokens), 1)
    earlier = jnp.where((node_col == node_row) & (along < above), 1.0, 0.0)
    rank_col = jnp.sum(earlier, axis=1, keepdims=True)
    slot_row = to_row(node_col * cap + rank_col)
    spread = jnp.where(
        lax.broadcasted_iota(jnp.int32, (slots, tokens), 0).astype(jnp.float32) == slot_row, 1.0, 0.0
    ).astype(jnp.bfloat16)

    def spread_out(i, pair):
        sendq[i] = dot(spread, pair).astype(jnp.bfloat16).reshape(n_row, cap, PAIR)

    qg[0] = q_ref[...]
    spread_out(0, q_ref[...])
    pl.semaphore_wait(barrier, n_row + n_col - 2)

    sent = []

    def send(copy):
        copy.start()
        sent.append(copy)
        return copy

    def q_copy(i):
        return copy_to(q_ref, qg.at[i], q_s.at[i], q_r.at[i], col=group(i))

    def branch_query(i, k):
        peer = (row + k) % n_row
        return copy_to(sendq.at[i, peer], brq.at[i, row], bq_s.at[i, k], bq_r.at[i, k], row=peer)

    def branch_out(i, k):
        peer = (row + k) % n_row
        return (
            copy_to(bro.at[i, peer], ret.at[i, row], bo_s.at[i, k], bo_r.at[i, k], row=peer),
            copy_to(bst.at[i, peer], rst.at[i, row], bs_s.at[i, k], bs_r.at[i, k], row=peer),
        )

    for i in range(1, n_col):
        send(q_copy(i))
    for k in range(1, n_row):
        branch_query(0, k).start()

    def flip(bit):
        return row + bit - 2 * bit * ((row // bit) % 2)

    mate, beside, below = flip(1), flip(2), flip(4)
    mate_copy = send(copy_to(root_ref, rootb.at[1], root_s.at[0], root_r.at[0], row=mate))
    rootb[0] = root_ref[...]

    first = 2 * (col % 2)

    def suffix_copy(h):
        return copy_to(suf_ref.at[:, pl.ds(h * HEAD_DIM, HEAD_DIM)], sbuf.at[col // 2], suf_s.at[h],
                       suf_r.at[col // 2], col=first + h)

    for h in range(2):
        @pl.when(first + h != col)
        def _():
            suffix_copy(h).start()

        @pl.when(first + h == col)
        def _():
            sbuf[col // 2] = suf_ref[:, h * HEAD_DIM:(h + 1) * HEAD_DIM]

    len_col = to_column(leaf_len_ref[...].astype(jnp.float32))
    key_at = lax.broadcasted_iota(jnp.int32, (1, leaf_keys), 1)
    key_leaf = (key_at // leaf_width).astype(jnp.float32)
    key_place = (col * leaf_width + key_at % leaf_width).astype(jnp.float32)
    rows32 = lax.broadcasted_iota(jnp.int32, (LEAF_ROW, leaf_keys), 0).astype(jnp.float32)
    key_len = jnp.sum(jnp.where(rows32 == key_leaf, len_col, 0.0), axis=0, keepdims=True)
    key_leaf = jnp.where(key_place < key_len, key_leaf, -1.0)
    leaf_col2 = jnp.concatenate([leaf_col, leaf_col], axis=0)

    loads[0].wait()
    loads[1].wait()

    def leaf_level(i):
        rows = stacked(qg[i])
        states = []
        for at in range(0, leaf_keys, KEY_STEP):
            states.append(state_of(
                rows, leafv[at:at + KEY_STEP, head_lanes(i)], leafv[at:at + KEY_STEP, value_lanes(i)],
                leaf_col2 == key_leaf[:, at:at + KEY_STEP],
            ))
        lm[i], ll[i], lo[i] = join(*states)

    def arrive(i, carry):
        @pl.when(i > 0)
        def _():
            q_copy(i).wait_recv()
            spread_out(i, qg[i])
            for k in range(1, n_row):
                branch_query(i, k).start()

        leaf_level(i)
        return carry

    lax.fori_loop(0, n_col, arrive, 0)
    beside_copy = send(copy_to(root_ref, rootb.at[2], root_s.at[1], root_r.at[1], row=beside))
    below_copy = send(copy_to(root_ref, rootb.at[4], root_s.at[2], root_r.at[2], row=below))
    for i in range(n_col):
        brq[i, row] = sendq[i, row]

    loads[2].wait()
    loads[3].wait()
    slot_at = lax.broadcasted_iota(jnp.int32, (n_row, cap, 128), 1)
    lane_at = lax.broadcasted_iota(jnp.int32, (n_row, cap, 128), 2)

    def branch_level(i, carry):
        for k in range(1, n_row):
            branch_query(i, k).wait_recv()
        rows = stacked(brq[i].reshape(slots, PAIR))
        states = []
        for at in range(0, branch_keys, KEY_STEP):
            place = col * branch_keys + at + lax.broadcasted_iota(jnp.int32, (1, KEY_STEP), 1)
            states.append(state_of(
                rows, branchv[at:at + KEY_STEP, head_lanes(i)], branchv[at:at + KEY_STEP, value_lanes(i)],
                place < branch_len_ref[...],
            ))
        highest, totals, summed = join(*states)
        for j in range(2):
            for at, column in ((j, highest), (2 + j, totals)):
                column = jnp.broadcast_to(column[j * slots:(j + 1) * slots], (slots, 128))
                line = jnp.sum(
                    jnp.where(slot_at == lane_at, column.reshape(n_row, cap, 128), 0.0), axis=1, keepdims=True
                )
                bst[i, :, at:at + 1, :] = line
                bst[i, :, at + 4:at + 5, :] = line
        summed = jnp.concatenate([summed[:slots], summed[slots:]], axis=1).astype(jnp.bfloat16)
        bro[i] = summed.reshape(n_row, cap, PAIR)
        for k in range(1, n_row):
            for copy in branch_out(i, k):
                copy.start()
        return carry

    lax.fori_loop(0, n_col, branch_level, 0)
    for i in range(n_col):
        ret[i, row] = bro[i, row]
        rst[i, row] = bst[i, row]

    half = root_ref.shape[0] // 2
    beside_copy.wait_recv()
    below_copy.wait_recv()
    low_copy = send(copy_to(rootb.at[2, pl.ds(0, half)], rootb.at[6, pl.ds(0, half)], fwd_s.at[0],
                            fwd_r.at[0], row=below))
    high_copy = send(copy_to(rootb.at[4, pl.ds(half, half)], rootb.at[6, pl.ds(half, half)], fwd_s.at[1],
                             fwd_r.at[1], row=beside))
    shared = [
        send(copy_to(rootb.at[2], rootb.at[3], fwd_s.at[2], fwd_r.at[2], row=mate)),
        send(copy_to(rootb.at[4], rootb.at[5], fwd_s.at[3], fwd_r.at[3], row=mate)),
    ]
    mate_copy.wait_recv()
    for copy in shared:
        copy.wait_recv()

    def root_level(i, blocks):
        keys, values = rootb[blocks, :, head_lanes(i)], rootb[blocks, :, value_lanes(i)]
        state = state_of(
            stacked(qg[i]), keys.reshape(-1, HEAD_DIM), values.reshape(-1, HEAD_DIM), None
        )
        lm[i], ll[i], lo[i] = join((lm[i], ll[i], lo[i]), state)

    def near_root(i, carry):
        root_level(i, slice(0, 6))
        return carry

    lax.fori_loop(0, n_col, near_root, 0)
    low_copy.wait_recv()
    high_copy.wait_recv()
    last = send(copy_to(rootb.at[6], rootb.at[7], fwd_s.at[4], fwd_r.at[4], row=mate))

    for i, local in ((0, 0), (1, n_col - 1)):
        @pl.when(col != local)
        def _():
            copy_to(suf_ref.at[:, pl.ds(0, HEAD_DIM)], sbuf.at[i], suf_s.at[0], suf_r.at[i],
                    col=(col + 1) % n_col).wait_recv()
    mask = (leaf_col2 == leaf_row) & (
        lax.broadcasted_iota(jnp.int32, (2 * tokens, tokens), 1)
        <= lax.broadcasted_iota(jnp.int32, (2 * tokens, tokens), 0) % tokens
    )
    own_state = state_of(stacked(q_ref[...]), sbuf[0], sbuf[1], mask)
    lm[0], ll[0], lo[0] = join((lm[0], ll[0], lo[0]), own_state)

    last.wait_recv()
    collect = jnp.where(
        lax.broadcasted_iota(jnp.int32, (tokens, slots), 1).astype(jnp.float32) == node_col * cap + rank_col,
        1.0, 0.0,
    ).astype(jnp.bfloat16)
    rank_here = along.astype(jnp.float32) == rank_col

    def final_copies(i):
        return (
            copy_to(fo.at[i], fin.at[i], f_s.at[i], f_r.at[i], col=group(i)),
            copy_to(fs.at[i], fins.at[i], fs_s.at[i], fs_r.at[i], col=group(i)),
        )

    def come_back(step, carry):
        i = (step + 1) % n_col
        root_level(i, slice(6, 8))
        for k in range(1, n_row):
            for copy in branch_out(i, k):
                copy.wait_recv()
        back = dot(collect, ret[i].reshape(slots, PAIR))
        stats = rst[i]

        def pick(index):
            found = jnp.zeros((tokens, 128), jnp.float32)
            for n in range(n_row):
                found = jnp.where(node_col == n, stats[n, index:index + 1, :], found)
            return jnp.sum(jnp.where(rank_here, found, 0.0), axis=1, keepdims=True)

        summed, lines = [], []
        for j in range(2):
            part = slice(j * tokens, (j + 1) * tokens)
            state = join(
                (lm[i, part], ll[i, part], lo[i, part]),
                (pick(j), pick(2 + j), back[:, j * HEAD_DIM:(j + 1) * HEAD_DIM]),
            )
            summed.append(state[2])
            lines += [to_row(state[0]), to_row(state[1])]
        fo[i] = jnp.concatenate(summed, axis=1).astype(jnp.bfloat16)
        fs[i] = jnp.concatenate(lines + lines, axis=0)

        @pl.when(i > 0)
        def _():
            for copy in final_copies(i):
                copy.start()

        return carry

    lax.fori_loop(0, n_col, come_back, 0)
    fin[0] = fo[0]
    fins[0] = fs[0]
    for i in range(1, n_col):
        for copy in final_copies(i):
            copy.wait_recv()
    for j in range(2):
        mine = None
        for i in range(n_col):
            lines = fins[i]
            other = (
                to_column(lines[2 * j:2 * j + 1]), to_column(lines[2 * j + 1:2 * j + 2]),
                fin[i, :, j * HEAD_DIM:(j + 1) * HEAD_DIM].astype(jnp.float32),
            )
            mine = other if mine is None else join(mine, other)
        out_ref[:, j * HEAD_DIM:(j + 1) * HEAD_DIM] = (mine[2] / mine[1]).astype(out_ref.dtype)

    for copy in sent:
        copy.wait_send()
    for h in range(2):
        @pl.when(first + h != col)
        def _():
            suffix_copy(h).wait_send()

    def drain(i, carry):
        for k in range(1, n_row):
            branch_query(i, k).wait_send()
            for copy in branch_out(i, k):
                copy.wait_send()

        @pl.when(i > 0)
        def _():
            for copy in final_copies(i):
                copy.wait_send()

        return carry

    lax.fori_loop(0, n_col, drain, 0)


def on_device_fused(
    queries, suffix_cache, suffix_leaf, leaf_parent, root_cache, branch_cache, branch_length, leaf_cache,
    leaf_length,
):
    n_row, n_col = lax.axis_size("row"), lax.axis_size("col")
    tokens = queries.shape[0]
    cap = tokens // 16 * (LEAF_ROW // n_row)
    slots = n_row * cap
    width = branch_cache.shape[2]
    branch = branch_cache.reshape(-1, width)
    leaf = leaf_cache.reshape(-1, width)
    bf16, f32 = jnp.bfloat16, jnp.float32
    dma = pltpu.SemaphoreType.DMA
    vmem = pltpu.VMEM
    scratch = [
        vmem((n_col, tokens, PAIR), bf16),
        vmem((2, tokens, HEAD_DIM), bf16),
        vmem((n_row,) + root_cache.shape, bf16),
        vmem(leaf.shape, bf16),
        vmem(branch.shape, bf16),
        vmem((n_col, n_row, cap, PAIR), bf16),
        vmem((n_col, n_row, cap, PAIR), bf16),
        vmem((n_col, n_row, cap, PAIR), bf16),
        vmem((n_col, n_row, 8, 128), f32),
        vmem((n_col, n_row, cap, PAIR), bf16),
        vmem((n_col, n_row, 8, 128), f32),
        vmem((KV_HEADS, 2 * tokens, 1), f32),
        vmem((KV_HEADS, 2 * tokens, 1), f32),
        vmem((KV_HEADS, 2 * tokens, HEAD_DIM), f32),
        vmem((KV_HEADS, tokens, PAIR), bf16),
        vmem((KV_HEADS, 8, tokens), f32),
        vmem((n_col, tokens, PAIR), bf16),
        vmem((n_col, 8, tokens), f32),
        dma((4,)),
        dma((n_col,)), dma((n_col,)),
        dma((2,)), dma((2,)),
        dma((3,)), dma((3,)),
        dma((5,)), dma((5,)),
        dma((n_col, n_row)), dma((n_col, n_row)),
        dma((n_col, n_row)), dma((n_col, n_row)),
        dma((n_col, n_row)), dma((n_col, n_row)),
        dma((n_col,)), dma((n_col,)),
        dma((n_col,)), dma((n_col,)),
    ]
    in_vmem = pl.BlockSpec(memory_space=pltpu.VMEM)
    anywhere = pl.BlockSpec(memory_space=pl.ANY)
    return pl.pallas_call(
        functools.partial(fused_kernel, n_row, n_col, cap),
        out_shape=jax.ShapeDtypeStruct(queries.shape, queries.dtype),
        in_specs=[in_vmem] * 7 + [anywhere] * 2,
        out_specs=in_vmem,
        scratch_shapes=scratch,
        compiler_params=pltpu.CompilerParams(
            collective_id=0, has_side_effects=True, vmem_limit_bytes=56 * 2**20
        ),
    )(
        queries, suffix_cache, suffix_leaf, leaf_parent, leaf_length.reshape(1, -1),
        branch_length.reshape(1, 1), root_cache, branch, leaf,
    )


def solution(mesh):
    in_specs = (
        P("row", "col"),
        P("row", "col"),
        P("row", None),
        P("row", None),
        P(("row", "col"), None),
        P("row", "col", None),
        P("row"),
        P("row", "col", None),
        P("row"),
    )
    out_specs = P("row", "col")
    sizes = dict(mesh.shape)
    body = on_device_fused if (sizes["row"], sizes["col"]) == (8, 4) else on_device
    return jax.shard_map(
        body, mesh=mesh, in_specs=in_specs, out_specs=out_specs, check_vma=False
    )
```

```python
import functools
import math

import jax
import jax.numpy as jnp
from jax import lax
from jax.experimental import pallas as pl
from jax.experimental.pallas import tpu as pltpu
from jax.sharding import PartitionSpec as P

HEADS = 8
KV_HEADS = 4
HEAD_DIM = 256
LEAF_ROW = 32


NEG = -1e30


def attend(queries, keys_values, usable):
    row_count = queries.shape[0]
    key_count = keys_values.shape[0]
    group_size = HEADS // KV_HEADS
    key_width = KV_HEADS * HEAD_DIM
    query_heads = queries.reshape(row_count, KV_HEADS, group_size, HEAD_DIM)
    key_heads = keys_values[:, :key_width].reshape(key_count, KV_HEADS, HEAD_DIM)
    value_heads = keys_values[:, key_width:].reshape(key_count, KV_HEADS, HEAD_DIM)
    scores = jnp.einsum(
        "rgjd,kgd->rgjk", query_heads, key_heads, preferred_element_type=jnp.float32
    ) * (1.0 / math.sqrt(HEAD_DIM))
    if usable is not None:
        key_mask = usable[:, None, None, :]
        scores = jnp.where(key_mask, scores, NEG)
    highest = jnp.max(scores, axis=-1)
    weights = jnp.exp(scores - highest[..., None])
    if usable is not None:
        weights = jnp.where(key_mask, weights, 0.0)
    totals = jnp.sum(weights, axis=-1)
    summed = jnp.einsum(
        "rgjk,kgd->rgjd",
        weights.astype(jnp.bfloat16),
        value_heads,
        preferred_element_type=jnp.float32,
    )
    return (
        highest.reshape(row_count, HEADS),
        totals.reshape(row_count, HEADS),
        summed.reshape(row_count, HEADS * HEAD_DIM),
    )


def merge_state(earlier, others):
    highest = jnp.maximum(earlier[0], others[0])
    keep_first = jnp.exp(earlier[0] - highest)
    keep_second = jnp.exp(others[0] - highest)
    totals = earlier[1] * keep_first + others[1] * keep_second
    summed = earlier[2] * jnp.repeat(keep_first, HEAD_DIM, axis=1) + others[2] * jnp.repeat(
        keep_second, HEAD_DIM, axis=1
    )
    return (highest, totals, summed)


def slice_heads(values, col_index, feature_width):
    per_slice = max(1, feature_width // HEAD_DIM)
    first_head = col_index * feature_width // HEAD_DIM
    chosen = lax.dynamic_slice_in_dim(values, first_head, per_slice, values.ndim - 1)
    return jnp.repeat(chosen, feature_width // per_slice, axis=values.ndim - 1)


def combine_columns(running):
    highest, totals, summed = running
    overall = lax.pmax(highest, "col")
    factors = jnp.exp(highest - overall)
    slice_sum = lax.psum_scatter(
        summed * jnp.repeat(factors, HEAD_DIM, axis=1), "col", scatter_dimension=1, tiled=True
    )
    overall_total = lax.psum(totals * factors, "col")
    return (overall, overall_total, slice_sum)


def on_device(
    queries,
    suffix_cache,
    suffix_leaf,
    leaf_parent,
    root_cache,
    branch_cache,
    branch_length,
    leaf_cache,
    leaf_length,
):
    col_count = lax.axis_size("col")
    row_count = lax.axis_size("row")
    col_index = lax.axis_index("col")
    full_queries, full_suffix = (
        lax.all_gather(queries, "col", axis=1, tiled=True),
        lax.all_gather(suffix_cache, "col", axis=1, tiled=True),
    )
    token_count = full_queries.shape[0]
    query_width = full_queries.shape[1]
    feature_width = queries.shape[1]
    leaf_local = suffix_leaf[0]
    positions = jnp.arange(token_count, dtype=jnp.int32)
    blank_state = (
        jnp.full((token_count, HEADS), NEG, jnp.float32),
        jnp.zeros((token_count, HEADS), jnp.float32),
        jnp.zeros((token_count, query_width), jnp.float32),
    )
    running = merge_state(
        blank_state,
        attend(full_queries, lax.all_gather(root_cache, "row", axis=0, tiled=True), None),
    )
    leaf_width = leaf_cache.shape[1]
    leaf_keys = leaf_cache.reshape(LEAF_ROW * leaf_width, leaf_cache.shape[2])
    key_slot = jnp.arange(LEAF_ROW * leaf_width, dtype=jnp.int32)
    key_leaf = key_slot // leaf_width
    key_place = col_index * leaf_width + key_slot % leaf_width
    leaf_ids = jnp.arange(LEAF_ROW, dtype=jnp.int32)
    key_live = jnp.any(
        (key_leaf[None, :] == leaf_ids[:, None]) & (key_place[None, :] < leaf_length[:, None]),
        axis=0,
    )
    usable = (leaf_local[:, None] == key_leaf[None, :]) & key_live[None, :]
    running = merge_state(running, attend(full_queries, leaf_keys, usable))
    suffix_width = token_count // col_count
    suffix_start = col_index * suffix_width
    suffix_keys = lax.dynamic_slice_in_dim(full_suffix, suffix_start, suffix_width, 0)
    suffix_owner = lax.dynamic_slice_in_dim(leaf_local, suffix_start, suffix_width, 0)
    suffix_place = suffix_start + jnp.arange(suffix_width, dtype=jnp.int32)
    usable = (leaf_local[:, None] == suffix_owner[None, :]) & (
        suffix_place[None, :] <= positions[:, None]
    )
    running = merge_state(running, attend(full_queries, suffix_keys, usable))
    parents = leaf_parent[0]
    token_node = jnp.sum(
        jnp.where(leaf_local[:, None] == leaf_ids[None, :], parents[None, :], 0), axis=1
    )
    node_ids = jnp.arange(row_count, dtype=jnp.int32)
    node_hits = (token_node[:, None] == node_ids[None, :]).astype(jnp.int32)
    rank_in_node = jnp.sum(node_hits * (jnp.cumsum(node_hits, axis=0) - 1), axis=1)
    capacity = token_count // 16 * (LEAF_ROW // row_count)
    slot_index = token_node * capacity + rank_in_node
    slot_token = (
        jnp.full((row_count * capacity,), token_count, jnp.int32).at[slot_index].set(positions)
    )
    padded = jnp.concatenate(
        [full_queries, jnp.zeros((1, query_width), full_queries.dtype)], axis=0
    )
    outgoing = padded[slot_token].reshape(row_count, capacity, query_width)
    branch_keys = branch_cache[0]
    branch_width = branch_keys.shape[0]
    branch_place = col_index * branch_width + jnp.arange(branch_width, dtype=jnp.int32)
    branch_usable = (branch_place < branch_length[0])[None, :]
    arrived = lax.all_to_all(outgoing, "row", split_axis=0, concat_axis=0, tiled=True)
    sources = arrived.shape[0]
    item_count = arrived.shape[1]
    flat_queries = arrived.reshape(sources * item_count, arrived.shape[2])
    highest, totals, summed = attend(flat_queries, branch_keys, branch_usable)
    returned = (
        lax.all_to_all(
            summed.reshape(sources, item_count, query_width),
            "row",
            split_axis=0,
            concat_axis=0,
            tiled=True,
        ),
        lax.all_to_all(
            highest.reshape(sources, item_count, HEADS),
            "row",
            split_axis=0,
            concat_axis=0,
            tiled=True,
        ),
        lax.all_to_all(
            totals.reshape(sources, item_count, HEADS),
            "row",
            split_axis=0,
            concat_axis=0,
            tiled=True,
        ),
    )
    back_sums = returned[0].reshape(row_count * capacity, returned[0].shape[2])[slot_index]
    back_peaks = returned[1].reshape(row_count * capacity, HEADS)[slot_index]
    back_totals = returned[2].reshape(row_count * capacity, HEADS)[slot_index]
    running = merge_state(running, (back_peaks, back_totals, back_sums))
    highest, totals, summed = combine_columns(running)
    output = summed / slice_heads(totals, col_index, feature_width)
    return output.astype(jnp.bfloat16)


LOW = -1e28
LOG2_SCALE = 1.0 / (math.sqrt(HEAD_DIM) * math.log(2.0))
KEY_WIDTH = KV_HEADS * HEAD_DIM
PAIR = HEADS // KV_HEADS * HEAD_DIM
KEY_STEP = 256
VALUE_STEP = 512
NT = (((1,), (1,)), ((), ()))
NN = (((1,), (0,)), ((), ()))


def dot(a, b, dims=NN, precision=None):
    return lax.dot_general(a, b, dims, precision=precision, preferred_element_type=jnp.float32)


def fold_lanes(values, operation):
    folded = values[:, :128]
    for at in range(128, values.shape[1], 128):
        folded = operation(folded, values[:, at:at + 128])
    return folded


def state_of(query_rows, keys, values, mask, count, held):
    rows = query_rows.shape[0]
    widest = None
    for at in range(0, count, KEY_STEP):
        span = min(KEY_STEP, count - at)
        scores = dot(query_rows, keys(at, span), NT)
        if mask is not None:
            scores = jnp.where(mask(at, span), scores, NEG)
        held[:rows, at:at + span] = scores
        folded = fold_lanes(scores, jnp.maximum)
        widest = folded if widest is None else jnp.maximum(widest, folded)
    highest = jnp.maximum(jnp.max(widest, axis=1, keepdims=True) * LOG2_SCALE, LOW)
    totals, summed = None, None
    for at in range(0, count, VALUE_STEP):
        span = min(VALUE_STEP, count - at)
        weights = jnp.exp2(held[:rows, at:at + span] * LOG2_SCALE - highest)
        folded = fold_lanes(weights, jnp.add)
        totals = folded if totals is None else totals + folded
        product = dot(weights.astype(jnp.bfloat16), values(at, span))
        summed = product if summed is None else summed + product
    return highest, jnp.sum(totals, axis=1, keepdims=True), summed


def join(first, second):
    highest = jnp.maximum(first[0], second[0])
    a, b = jnp.exp2(first[0] - highest), jnp.exp2(second[0] - highest)
    return highest, first[1] * a + second[1] * b, first[2] * a + second[2] * b


def stacked(pair):
    return jnp.concatenate([pair[:, :HEAD_DIM], pair[:, HEAD_DIM:]], axis=0)


def fused_kernel(
    n_row, n_col, cap,
    q_ref, suf_ref, leaf_of_ref, parent_ref, leaf_len_ref, branch_len_ref, root_ref, branch_ref, leaf_ref,
    out_ref,
    qg, sbuf, rootb, leafv, branchv, sendq, brq, bro, bst, ret, rst, lm, ll, lo, fo, fs, fin, fins, held,
    load_sem, q_s, q_r, suf_s, suf_r, root_s, root_r, fwd_s, fwd_r, bq_s, bq_r, bo_s, bo_r, bs_s, bs_r,
    f_s, f_r, fs_s, fs_r,
):
    row, col = lax.axis_index("row"), lax.axis_index("col")
    tokens = q_ref.shape[0]
    slots = n_row * cap
    branch_keys, leaf_keys = branchv.shape[0], leafv.shape[0]
    leaf_width = leaf_keys // LEAF_ROW

    def copy_to(src, dst, s, r, **where):
        return pltpu.make_async_remote_copy(
            src_ref=src, dst_ref=dst, send_sem=s, recv_sem=r, device_id=where,
            device_id_type=pl.DeviceIdType.MESH,
        )

    def group(i):
        return (col + i) % 2 + 2 * ((col // 2 + i // 2) % 2)

    def head_lanes(i):
        return pl.ds(pl.multiple_of(group(i) * HEAD_DIM, HEAD_DIM), HEAD_DIM)

    def value_lanes(i):
        return pl.ds(pl.multiple_of(KEY_WIDTH + group(i) * HEAD_DIM, HEAD_DIM), HEAD_DIM)

    loads = []
    for i, (src, dst) in enumerate(((leaf_ref, leafv), (branch_ref, branchv))):
        step = dst.shape[0] // 2
        for j in range(2):
            part = pl.ds(j * step, step)
            loads.append(pltpu.make_async_copy(src.at[part], dst.at[part], load_sem.at[2 * i + j]))
    for load in loads:
        load.start()

    barrier = pltpu.get_barrier_semaphore()
    for k in range(1, n_row):
        pl.semaphore_signal(barrier, inc=1, device_id={"row": (row + k) % n_row},
                            device_id_type=pl.DeviceIdType.MESH)
    for k in range(1, n_col):
        pl.semaphore_signal(barrier, inc=1, device_id={"col": (col + k) % n_col},
                            device_id_type=pl.DeviceIdType.MESH)

    def eye(n):
        return lax.broadcasted_iota(jnp.int32, (n, n), 0) == lax.broadcasted_iota(jnp.int32, (n, n), 1)

    def to_column(values):
        return jnp.sum(jnp.where(eye(values.shape[1]), values, 0.0), axis=1, keepdims=True)

    def to_row(values):
        return jnp.sum(jnp.where(eye(values.shape[0]), values, 0.0), axis=0, keepdims=True)

    leaf_row = leaf_of_ref[...].astype(jnp.float32)
    leaf_col = to_column(leaf_row)
    parent_row = parent_ref[...].astype(jnp.float32)
    leaf_iota = lax.broadcasted_iota(jnp.int32, (tokens, LEAF_ROW), 1).astype(jnp.float32)
    node_col = jnp.sum(jnp.where(leaf_col == leaf_iota, parent_row, 0.0), axis=1, keepdims=True)
    node_row = to_row(node_col)
    above = lax.broadcasted_iota(jnp.int32, (tokens, tokens), 0)
    along = lax.broadcasted_iota(jnp.int32, (tokens, tokens), 1)
    earlier = jnp.where((node_col == node_row) & (along < above), 1.0, 0.0)
    rank_col = jnp.sum(earlier, axis=1, keepdims=True)
    slot_row = to_row(node_col * cap + rank_col)
    spread = jnp.where(
        lax.broadcasted_iota(jnp.int32, (slots, tokens), 0).astype(jnp.float32) == slot_row, 1.0, 0.0
    ).astype(jnp.bfloat16)

    def spread_out(i, pair):
        sendq[i] = dot(spread, pair).astype(jnp.bfloat16).reshape(n_row, cap, PAIR)

    qg[0] = q_ref[...]
    spread_out(0, q_ref[...])
    pl.semaphore_wait(barrier, n_row + n_col - 2)

    sent = []

    def send(copy):
        copy.start()
        sent.append(copy)
        return copy

    def q_copy(i):
        return copy_to(q_ref, qg.at[i], q_s.at[i], q_r.at[i], col=group(i))

    def branch_query(i, k):
        peer = (row + k) % n_row
        return copy_to(sendq.at[i, peer], brq.at[i, row], bq_s.at[i, k], bq_r.at[i, k], row=peer)

    def branch_out(i, k):
        peer = (row + k) % n_row
        return (
            copy_to(bro.at[i, peer], ret.at[i, row], bo_s.at[i, k], bo_r.at[i, k], row=peer),
            copy_to(bst.at[i, peer], rst.at[i, row], bs_s.at[i, k], bs_r.at[i, k], row=peer),
        )

    for i in range(1, n_col):
        send(q_copy(i))
    for k in range(1, n_row):
        branch_query(0, k).start()

    def flip(bit):
        return row + bit - 2 * bit * ((row // bit) % 2)

    mate, beside, below = flip(1), flip(2), flip(4)
    mate_copy = send(copy_to(root_ref, rootb.at[1], root_s.at[0], root_r.at[0], row=mate))
    rootb[0] = root_ref[...]

    first = 2 * (col % 2)

    def suffix_copy(h):
        return copy_to(suf_ref.at[:, pl.ds(h * HEAD_DIM, HEAD_DIM)], sbuf.at[col // 2], suf_s.at[h],
                       suf_r.at[col // 2], col=first + h)

    for h in range(2):
        @pl.when(first + h != col)
        def _():
            suffix_copy(h).start()

        @pl.when(first + h == col)
        def _():
            sbuf[col // 2] = suf_ref[:, h * HEAD_DIM:(h + 1) * HEAD_DIM]

    len_col = to_column(leaf_len_ref[...].astype(jnp.float32))
    key_at = lax.broadcasted_iota(jnp.int32, (1, leaf_keys), 1)
    key_leaf = (key_at // leaf_width).astype(jnp.float32)
    key_place = (col * leaf_width + key_at % leaf_width).astype(jnp.float32)
    rows32 = lax.broadcasted_iota(jnp.int32, (LEAF_ROW, leaf_keys), 0).astype(jnp.float32)
    key_len = jnp.sum(jnp.where(rows32 == key_leaf, len_col, 0.0), axis=0, keepdims=True)
    key_leaf = jnp.where(key_place < key_len, key_leaf, -1.0)
    leaf_col2 = jnp.concatenate([leaf_col, leaf_col], axis=0)

    loads[0].wait()
    loads[1].wait()

    def leaf_level(i):
        rows = stacked(qg[i])
        lm[i], ll[i], lo[i] = state_of(
            rows,
            lambda at, span: leafv[at:at + span, head_lanes(i)],
            lambda at, span: leafv[at:at + span, value_lanes(i)],
            lambda at, span: leaf_col2 == key_leaf[:, at:at + span],
            leaf_keys, held,
        )

    def arrive(i, carry):
        @pl.when(i > 0)
        def _():
            q_copy(i).wait_recv()
            spread_out(i, qg[i])
            for k in range(1, n_row):
                branch_query(i, k).start()

        leaf_level(i)
        return carry

    lax.fori_loop(0, n_col, arrive, 0)
    beside_copy = send(copy_to(root_ref, rootb.at[2], root_s.at[1], root_r.at[1], row=beside))
    below_copy = send(copy_to(root_ref, rootb.at[4], root_s.at[2], root_r.at[2], row=below))
    for i in range(n_col):
        brq[i, row] = sendq[i, row]

    loads[2].wait()
    loads[3].wait()
    slot_at = lax.broadcasted_iota(jnp.int32, (n_row, cap, 128), 1)
    lane_at = lax.broadcasted_iota(jnp.int32, (n_row, cap, 128), 2)

    def branch_level(i, carry):
        for k in range(1, n_row):
            branch_query(i, k).wait_recv()
        rows = stacked(brq[i].reshape(slots, PAIR))

        def usable(at, span):
            place = col * branch_keys + at + lax.broadcasted_iota(jnp.int32, (1, span), 1)
            return place < branch_len_ref[...]

        highest, totals, summed = state_of(
            rows,
            lambda at, span: branchv[at:at + span, head_lanes(i)],
            lambda at, span: branchv[at:at + span, value_lanes(i)],
            usable, branch_keys, held,
        )
        for j in range(2):
            for at, column in ((j, highest), (2 + j, totals)):
                column = jnp.broadcast_to(column[j * slots:(j + 1) * slots], (slots, 128))
                line = jnp.sum(
                    jnp.where(slot_at == lane_at, column.reshape(n_row, cap, 128), 0.0), axis=1, keepdims=True
                )
                bst[i, :, at:at + 1, :] = line
                bst[i, :, at + 4:at + 5, :] = line
        summed = jnp.concatenate([summed[:slots], summed[slots:]], axis=1).astype(jnp.bfloat16)
        bro[i] = summed.reshape(n_row, cap, PAIR)
        for k in range(1, n_row):
            for copy in branch_out(i, k):
                copy.start()
        return carry

    lax.fori_loop(0, n_col, branch_level, 0)
    for i in range(n_col):
        ret[i, row] = bro[i, row]
        rst[i, row] = bst[i, row]

    half = root_ref.shape[0] // 2
    beside_copy.wait_recv()
    below_copy.wait_recv()
    low_copy = send(copy_to(rootb.at[2, pl.ds(0, half)], rootb.at[6, pl.ds(0, half)], fwd_s.at[0],
                            fwd_r.at[0], row=below))
    high_copy = send(copy_to(rootb.at[4, pl.ds(half, half)], rootb.at[6, pl.ds(half, half)], fwd_s.at[1],
                             fwd_r.at[1], row=beside))
    shared = [
        send(copy_to(rootb.at[2], rootb.at[3], fwd_s.at[2], fwd_r.at[2], row=mate)),
        send(copy_to(rootb.at[4], rootb.at[5], fwd_s.at[3], fwd_r.at[3], row=mate)),
    ]
    mate_copy.wait_recv()
    for copy in shared:
        copy.wait_recv()

    def root_level(i, blocks):
        size = root_ref.shape[0]

        def part(lanes):
            def take(at, span):
                chosen = slice(blocks.start + at // size, blocks.start + (at + span) // size)
                return rootb[chosen, :, lanes].reshape(span, HEAD_DIM)
            return take

        state = state_of(
            stacked(qg[i]), part(head_lanes(i)), part(value_lanes(i)), None,
            (blocks.stop - blocks.start) * size, held,
        )
        lm[i], ll[i], lo[i] = join((lm[i], ll[i], lo[i]), state)

    def near_root(i, carry):
        root_level(i, slice(0, 6))
        return carry

    lax.fori_loop(0, n_col, near_root, 0)
    low_copy.wait_recv()
    high_copy.wait_recv()
    last = send(copy_to(rootb.at[6], rootb.at[7], fwd_s.at[4], fwd_r.at[4], row=mate))

    for i, local in ((0, 0), (1, n_col - 1)):
        @pl.when(col != local)
        def _():
            copy_to(suf_ref.at[:, pl.ds(0, HEAD_DIM)], sbuf.at[i], suf_s.at[0], suf_r.at[i],
                    col=(col + 1) % n_col).wait_recv()
    mask = (leaf_col2 == leaf_row) & (
        lax.broadcasted_iota(jnp.int32, (2 * tokens, tokens), 1)
        <= lax.broadcasted_iota(jnp.int32, (2 * tokens, tokens), 0) % tokens
    )
    own_state = state_of(
        stacked(q_ref[...]), lambda at, span: sbuf[0], lambda at, span: sbuf[1], lambda at, span: mask,
        tokens, held,
    )
    lm[0], ll[0], lo[0] = join((lm[0], ll[0], lo[0]), own_state)

    last.wait_recv()
    collect = jnp.where(
        lax.broadcasted_iota(jnp.int32, (tokens, slots), 1).astype(jnp.float32) == node_col * cap + rank_col,
        1.0, 0.0,
    ).astype(jnp.bfloat16)
    rank_here = along.astype(jnp.float32) == rank_col

    def final_copies(i):
        return (
            copy_to(fo.at[i], fin.at[i], f_s.at[i], f_r.at[i], col=group(i)),
            copy_to(fs.at[i], fins.at[i], fs_s.at[i], fs_r.at[i], col=group(i)),
        )

    def come_back(step, carry):
        i = (step + 1) % n_col
        root_level(i, slice(6, 8))
        for k in range(1, n_row):
            for copy in branch_out(i, k):
                copy.wait_recv()
        back = dot(collect, ret[i].reshape(slots, PAIR))
        stats = rst[i]

        def pick(index):
            found = jnp.zeros((tokens, 128), jnp.float32)
            for n in range(n_row):
                found = jnp.where(node_col == n, stats[n, index:index + 1, :], found)
            return jnp.sum(jnp.where(rank_here, found, 0.0), axis=1, keepdims=True)

        summed, lines = [], []
        for j in range(2):
            part = slice(j * tokens, (j + 1) * tokens)
            state = join(
                (lm[i, part], ll[i, part], lo[i, part]),
                (pick(j), pick(2 + j), back[:, j * HEAD_DIM:(j + 1) * HEAD_DIM]),
            )
            summed.append(state[2])
            lines += [to_row(state[0]), to_row(state[1])]
        fo[i] = jnp.concatenate(summed, axis=1).astype(jnp.bfloat16)
        fs[i] = jnp.concatenate(lines + lines, axis=0)

        @pl.when(i > 0)
        def _():
            for copy in final_copies(i):
                copy.start()

        return carry

    lax.fori_loop(0, n_col, come_back, 0)
    fin[0] = fo[0]
    fins[0] = fs[0]
    for i in range(1, n_col):
        for copy in final_copies(i):
            copy.wait_recv()
    for j in range(2):
        mine = None
        for i in range(n_col):
            lines = fins[i]
            other = (
                to_column(lines[2 * j:2 * j + 1]), to_column(lines[2 * j + 1:2 * j + 2]),
                fin[i, :, j * HEAD_DIM:(j + 1) * HEAD_DIM].astype(jnp.float32),
            )
            mine = other if mine is None else join(mine, other)
        out_ref[:, j * HEAD_DIM:(j + 1) * HEAD_DIM] = (mine[2] / mine[1]).astype(out_ref.dtype)

    for copy in sent:
        copy.wait_send()
    for h in range(2):
        @pl.when(first + h != col)
        def _():
            suffix_copy(h).wait_send()

    def drain(i, carry):
        for k in range(1, n_row):
            branch_query(i, k).wait_send()
            for copy in branch_out(i, k):
                copy.wait_send()

        @pl.when(i > 0)
        def _():
            for copy in final_copies(i):
                copy.wait_send()

        return carry

    lax.fori_loop(0, n_col, drain, 0)


def on_device_fused(
    queries, suffix_cache, suffix_leaf, leaf_parent, root_cache, branch_cache, branch_length, leaf_cache,
    leaf_length,
):
    n_row, n_col = lax.axis_size("row"), lax.axis_size("col")
    tokens = queries.shape[0]
    cap = tokens // 16 * (LEAF_ROW // n_row)
    slots = n_row * cap
    width = branch_cache.shape[2]
    branch = branch_cache.reshape(-1, width)
    leaf = leaf_cache.reshape(-1, width)
    bf16, f32 = jnp.bfloat16, jnp.float32
    dma = pltpu.SemaphoreType.DMA
    vmem = pltpu.VMEM
    scratch = [
        vmem((n_col, tokens, PAIR), bf16),
        vmem((2, tokens, HEAD_DIM), bf16),
        vmem((n_row,) + root_cache.shape, bf16),
        vmem(leaf.shape, bf16),
        vmem(branch.shape, bf16),
        vmem((n_col, n_row, cap, PAIR), bf16),
        vmem((n_col, n_row, cap, PAIR), bf16),
        vmem((n_col, n_row, cap, PAIR), bf16),
        vmem((n_col, n_row, 8, 128), f32),
        vmem((n_col, n_row, cap, PAIR), bf16),
        vmem((n_col, n_row, 8, 128), f32),
        vmem((KV_HEADS, 2 * tokens, 1), f32),
        vmem((KV_HEADS, 2 * tokens, 1), f32),
        vmem((KV_HEADS, 2 * tokens, HEAD_DIM), f32),
        vmem((KV_HEADS, tokens, PAIR), bf16),
        vmem((KV_HEADS, 8, tokens), f32),
        vmem((n_col, tokens, PAIR), bf16),
        vmem((n_col, 8, tokens), f32),
        vmem((max(2 * slots, 2 * tokens), max(branch.shape[0], leaf.shape[0])), f32),
        dma((4,)),
        dma((n_col,)), dma((n_col,)),
        dma((2,)), dma((2,)),
        dma((3,)), dma((3,)),
        dma((5,)), dma((5,)),
        dma((n_col, n_row)), dma((n_col, n_row)),
        dma((n_col, n_row)), dma((n_col, n_row)),
        dma((n_col, n_row)), dma((n_col, n_row)),
        dma((n_col,)), dma((n_col,)),
        dma((n_col,)), dma((n_col,)),
    ]
    in_vmem = pl.BlockSpec(memory_space=pltpu.VMEM)
    anywhere = pl.BlockSpec(memory_space=pl.ANY)
    return pl.pallas_call(
        functools.partial(fused_kernel, n_row, n_col, cap),
        out_shape=jax.ShapeDtypeStruct(queries.shape, queries.dtype),
        in_specs=[in_vmem] * 7 + [anywhere] * 2,
        out_specs=in_vmem,
        scratch_shapes=scratch,
        compiler_params=pltpu.CompilerParams(
            collective_id=0, has_side_effects=True, vmem_limit_bytes=56 * 2**20
        ),
    )(
        queries, suffix_cache, suffix_leaf, leaf_parent, leaf_length.reshape(1, -1),
        branch_length.reshape(1, 1), root_cache, branch, leaf,
    )


def solution(mesh):
    in_specs = (
        P("row", "col"),
        P("row", "col"),
        P("row", None),
        P("row", None),
        P(("row", "col"), None),
        P("row", "col", None),
        P("row"),
        P("row", "col", None),
        P("row"),
    )
    out_specs = P("row", "col")
    sizes = dict(mesh.shape)
    body = on_device_fused if (sizes["row"], sizes["col"]) == (8, 4) else on_device
    return jax.shard_map(
        body, mesh=mesh, in_specs=in_specs, out_specs=out_specs, check_vma=False
    )
```

```python
import functools
import math

import jax
import jax.numpy as jnp
from jax import lax
from jax.experimental import pallas as pl
from jax.experimental.pallas import tpu as pltpu
from jax.sharding import PartitionSpec as P

HEADS = 8
KV_HEADS = 4
HEAD_DIM = 256
LEAF_ROW = 32


NEG = -1e30


def attend(queries, keys_values, usable):
    row_count = queries.shape[0]
    key_count = keys_values.shape[0]
    group_size = HEADS // KV_HEADS
    key_width = KV_HEADS * HEAD_DIM
    query_heads = queries.reshape(row_count, KV_HEADS, group_size, HEAD_DIM)
    key_heads = keys_values[:, :key_width].reshape(key_count, KV_HEADS, HEAD_DIM)
    value_heads = keys_values[:, key_width:].reshape(key_count, KV_HEADS, HEAD_DIM)
    scores = jnp.einsum(
        "rgjd,kgd->rgjk", query_heads, key_heads, preferred_element_type=jnp.float32
    ) * (1.0 / math.sqrt(HEAD_DIM))
    if usable is not None:
        key_mask = usable[:, None, None, :]
        scores = jnp.where(key_mask, scores, NEG)
    highest = jnp.max(scores, axis=-1)
    weights = jnp.exp(scores - highest[..., None])
    if usable is not None:
        weights = jnp.where(key_mask, weights, 0.0)
    totals = jnp.sum(weights, axis=-1)
    summed = jnp.einsum(
        "rgjk,kgd->rgjd",
        weights.astype(jnp.bfloat16),
        value_heads,
        preferred_element_type=jnp.float32,
    )
    return (
        highest.reshape(row_count, HEADS),
        totals.reshape(row_count, HEADS),
        summed.reshape(row_count, HEADS * HEAD_DIM),
    )


def merge_state(earlier, others):
    highest = jnp.maximum(earlier[0], others[0])
    keep_first = jnp.exp(earlier[0] - highest)
    keep_second = jnp.exp(others[0] - highest)
    totals = earlier[1] * keep_first + others[1] * keep_second
    summed = earlier[2] * jnp.repeat(keep_first, HEAD_DIM, axis=1) + others[2] * jnp.repeat(
        keep_second, HEAD_DIM, axis=1
    )
    return (highest, totals, summed)


def slice_heads(values, col_index, feature_width):
    per_slice = max(1, feature_width // HEAD_DIM)
    first_head = col_index * feature_width // HEAD_DIM
    chosen = lax.dynamic_slice_in_dim(values, first_head, per_slice, values.ndim - 1)
    return jnp.repeat(chosen, feature_width // per_slice, axis=values.ndim - 1)


def combine_columns(running):
    highest, totals, summed = running
    overall = lax.pmax(highest, "col")
    factors = jnp.exp(highest - overall)
    slice_sum = lax.psum_scatter(
        summed * jnp.repeat(factors, HEAD_DIM, axis=1), "col", scatter_dimension=1, tiled=True
    )
    overall_total = lax.psum(totals * factors, "col")
    return (overall, overall_total, slice_sum)


def on_device(
    queries,
    suffix_cache,
    suffix_leaf,
    leaf_parent,
    root_cache,
    branch_cache,
    branch_length,
    leaf_cache,
    leaf_length,
):
    col_count = lax.axis_size("col")
    row_count = lax.axis_size("row")
    col_index = lax.axis_index("col")
    full_queries, full_suffix = (
        lax.all_gather(queries, "col", axis=1, tiled=True),
        lax.all_gather(suffix_cache, "col", axis=1, tiled=True),
    )
    token_count = full_queries.shape[0]
    query_width = full_queries.shape[1]
    feature_width = queries.shape[1]
    leaf_local = suffix_leaf[0]
    positions = jnp.arange(token_count, dtype=jnp.int32)
    blank_state = (
        jnp.full((token_count, HEADS), NEG, jnp.float32),
        jnp.zeros((token_count, HEADS), jnp.float32),
        jnp.zeros((token_count, query_width), jnp.float32),
    )
    running = merge_state(
        blank_state,
        attend(full_queries, lax.all_gather(root_cache, "row", axis=0, tiled=True), None),
    )
    leaf_width = leaf_cache.shape[1]
    leaf_keys = leaf_cache.reshape(LEAF_ROW * leaf_width, leaf_cache.shape[2])
    key_slot = jnp.arange(LEAF_ROW * leaf_width, dtype=jnp.int32)
    key_leaf = key_slot // leaf_width
    key_place = col_index * leaf_width + key_slot % leaf_width
    leaf_ids = jnp.arange(LEAF_ROW, dtype=jnp.int32)
    key_live = jnp.any(
        (key_leaf[None, :] == leaf_ids[:, None]) & (key_place[None, :] < leaf_length[:, None]),
        axis=0,
    )
    usable = (leaf_local[:, None] == key_leaf[None, :]) & key_live[None, :]
    running = merge_state(running, attend(full_queries, leaf_keys, usable))
    suffix_width = token_count // col_count
    suffix_start = col_index * suffix_width
    suffix_keys = lax.dynamic_slice_in_dim(full_suffix, suffix_start, suffix_width, 0)
    suffix_owner = lax.dynamic_slice_in_dim(leaf_local, suffix_start, suffix_width, 0)
    suffix_place = suffix_start + jnp.arange(suffix_width, dtype=jnp.int32)
    usable = (leaf_local[:, None] == suffix_owner[None, :]) & (
        suffix_place[None, :] <= positions[:, None]
    )
    running = merge_state(running, attend(full_queries, suffix_keys, usable))
    parents = leaf_parent[0]
    token_node = jnp.sum(
        jnp.where(leaf_local[:, None] == leaf_ids[None, :], parents[None, :], 0), axis=1
    )
    node_ids = jnp.arange(row_count, dtype=jnp.int32)
    node_hits = (token_node[:, None] == node_ids[None, :]).astype(jnp.int32)
    rank_in_node = jnp.sum(node_hits * (jnp.cumsum(node_hits, axis=0) - 1), axis=1)
    capacity = token_count // 16 * (LEAF_ROW // row_count)
    slot_index = token_node * capacity + rank_in_node
    slot_token = (
        jnp.full((row_count * capacity,), token_count, jnp.int32).at[slot_index].set(positions)
    )
    padded = jnp.concatenate(
        [full_queries, jnp.zeros((1, query_width), full_queries.dtype)], axis=0
    )
    outgoing = padded[slot_token].reshape(row_count, capacity, query_width)
    branch_keys = branch_cache[0]
    branch_width = branch_keys.shape[0]
    branch_place = col_index * branch_width + jnp.arange(branch_width, dtype=jnp.int32)
    branch_usable = (branch_place < branch_length[0])[None, :]
    arrived = lax.all_to_all(outgoing, "row", split_axis=0, concat_axis=0, tiled=True)
    sources = arrived.shape[0]
    item_count = arrived.shape[1]
    flat_queries = arrived.reshape(sources * item_count, arrived.shape[2])
    highest, totals, summed = attend(flat_queries, branch_keys, branch_usable)
    returned = (
        lax.all_to_all(
            summed.reshape(sources, item_count, query_width),
            "row",
            split_axis=0,
            concat_axis=0,
            tiled=True,
        ),
        lax.all_to_all(
            highest.reshape(sources, item_count, HEADS),
            "row",
            split_axis=0,
            concat_axis=0,
            tiled=True,
        ),
        lax.all_to_all(
            totals.reshape(sources, item_count, HEADS),
            "row",
            split_axis=0,
            concat_axis=0,
            tiled=True,
        ),
    )
    back_sums = returned[0].reshape(row_count * capacity, returned[0].shape[2])[slot_index]
    back_peaks = returned[1].reshape(row_count * capacity, HEADS)[slot_index]
    back_totals = returned[2].reshape(row_count * capacity, HEADS)[slot_index]
    running = merge_state(running, (back_peaks, back_totals, back_sums))
    highest, totals, summed = combine_columns(running)
    output = summed / slice_heads(totals, col_index, feature_width)
    return output.astype(jnp.bfloat16)


LOW = -1e28
LOG2_SCALE = 1.0 / (math.sqrt(HEAD_DIM) * math.log(2.0))
KEY_WIDTH = KV_HEADS * HEAD_DIM
PAIR = HEADS // KV_HEADS * HEAD_DIM
KEY_STEP = 256
VALUE_STEP = 512
NT = (((1,), (1,)), ((), ()))
NN = (((1,), (0,)), ((), ()))


def dot(a, b, dims=NN, precision=None):
    return lax.dot_general(a, b, dims, precision=precision, preferred_element_type=jnp.float32)


def fold_lanes(values, operation):
    folded = values[:, :128]
    for at in range(128, values.shape[1], 128):
        folded = operation(folded, values[:, at:at + 128])
    return folded


def state_of(query_rows, keys, values, mask, count, held):
    rows = query_rows.shape[0]
    widest = None
    for at in range(0, count, KEY_STEP):
        span = min(KEY_STEP, count - at)
        scores = dot(query_rows, keys(at, span), NT)
        if mask is not None:
            scores = jnp.where(mask(at, span), scores, NEG)
        held[:rows, at:at + span] = scores
        folded = fold_lanes(scores, jnp.maximum)
        widest = folded if widest is None else jnp.maximum(widest, folded)
    highest = jnp.maximum(jnp.max(widest, axis=1, keepdims=True) * LOG2_SCALE, LOW)
    totals, summed = None, None
    for at in range(0, count, VALUE_STEP):
        span = min(VALUE_STEP, count - at)
        weights = jnp.exp2(held[:rows, at:at + span] * LOG2_SCALE - highest)
        folded = fold_lanes(weights, jnp.add)
        totals = folded if totals is None else totals + folded
        product = dot(weights.astype(jnp.bfloat16), values(at, span))
        summed = product if summed is None else summed + product
    return highest, jnp.sum(totals, axis=1, keepdims=True), summed


def join(first, second):
    highest = jnp.maximum(first[0], second[0])
    a, b = jnp.exp2(first[0] - highest), jnp.exp2(second[0] - highest)
    return highest, first[1] * a + second[1] * b, first[2] * a + second[2] * b


def stacked(pair):
    return jnp.concatenate([pair[:, :HEAD_DIM], pair[:, HEAD_DIM:]], axis=0)


def fused_kernel(
    n_row, n_col, cap,
    q_ref, suf_ref, leaf_of_ref, parent_ref, leaf_len_ref, branch_len_ref, root_ref, branch_ref, leaf_ref,
    out_ref,
    qg, sbuf, rootb, leafv, branchv, sendq, brq, bro, bst, ret, rst, lm, ll, lo, fo, fs, fin, fins, held,
    load_sem, q_s, q_r, suf_s, suf_r, root_s, root_r, fwd_s, fwd_r, bq_s, bq_r, bo_s, bo_r, bs_s, bs_r,
    f_s, f_r, fs_s, fs_r,
):
    row, col = lax.axis_index("row"), lax.axis_index("col")
    tokens = q_ref.shape[0]
    slots = n_row * cap
    branch_keys, leaf_keys = branchv.shape[0], leafv.shape[0]
    leaf_width = leaf_keys // LEAF_ROW

    def copy_to(src, dst, s, r, **where):
        return pltpu.make_async_remote_copy(
            src_ref=src, dst_ref=dst, send_sem=s, recv_sem=r, device_id=where,
            device_id_type=pl.DeviceIdType.MESH,
        )

    def group(i):
        return (col + i) % 2 + 2 * ((col // 2 + i // 2) % 2)

    def head_lanes(i):
        return pl.ds(pl.multiple_of(group(i) * HEAD_DIM, HEAD_DIM), HEAD_DIM)

    def value_lanes(i):
        return pl.ds(pl.multiple_of(KEY_WIDTH + group(i) * HEAD_DIM, HEAD_DIM), HEAD_DIM)

    loads = []
    for i, (src, dst) in enumerate(((leaf_ref, leafv), (branch_ref, branchv))):
        step = dst.shape[0] // 2
        for j in range(2):
            part = pl.ds(j * step, step)
            loads.append(pltpu.make_async_copy(src.at[part], dst.at[part], load_sem.at[2 * i + j]))
    for load in loads:
        load.start()

    barrier = pltpu.get_barrier_semaphore()
    for k in range(1, n_row):
        pl.semaphore_signal(barrier, inc=1, device_id={"row": (row + k) % n_row},
                            device_id_type=pl.DeviceIdType.MESH)
    for k in range(1, n_col):
        pl.semaphore_signal(barrier, inc=1, device_id={"col": (col + k) % n_col},
                            device_id_type=pl.DeviceIdType.MESH)

    def eye(n):
        return lax.broadcasted_iota(jnp.int32, (n, n), 0) == lax.broadcasted_iota(jnp.int32, (n, n), 1)

    def to_column(values):
        return jnp.sum(jnp.where(eye(values.shape[1]), values, 0.0), axis=1, keepdims=True)

    def to_row(values):
        return jnp.sum(jnp.where(eye(values.shape[0]), values, 0.0), axis=0, keepdims=True)

    leaf_row = leaf_of_ref[...].astype(jnp.float32)
    leaf_col = to_column(leaf_row)
    parent_row = parent_ref[...].astype(jnp.float32)
    leaf_iota = lax.broadcasted_iota(jnp.int32, (tokens, LEAF_ROW), 1).astype(jnp.float32)
    node_col = jnp.sum(jnp.where(leaf_col == leaf_iota, parent_row, 0.0), axis=1, keepdims=True)
    node_row = to_row(node_col)
    above = lax.broadcasted_iota(jnp.int32, (tokens, tokens), 0)
    along = lax.broadcasted_iota(jnp.int32, (tokens, tokens), 1)
    earlier = jnp.where((node_col == node_row) & (along < above), 1.0, 0.0)
    rank_col = jnp.sum(earlier, axis=1, keepdims=True)
    slot_row = to_row(node_col * cap + rank_col)
    spread = jnp.where(
        lax.broadcasted_iota(jnp.int32, (slots, tokens), 0).astype(jnp.float32) == slot_row, 1.0, 0.0
    ).astype(jnp.bfloat16)

    def spread_out(i, pair):
        sendq[i] = dot(spread, pair).astype(jnp.bfloat16).reshape(n_row, cap, PAIR)

    qg[0] = q_ref[...]
    spread_out(0, q_ref[...])
    pl.semaphore_wait(barrier, n_row + n_col - 2)

    sent = []

    def send(copy):
        copy.start()
        sent.append(copy)
        return copy

    def q_copy(i):
        return copy_to(q_ref, qg.at[i], q_s.at[i], q_r.at[i], col=group(i))

    def branch_query(i, k):
        peer = (row + k) % n_row
        return copy_to(sendq.at[i, peer], brq.at[i, row], bq_s.at[i, k], bq_r.at[i, k], row=peer)

    def branch_out(i, k):
        peer = (row + k) % n_row
        return (
            copy_to(bro.at[i, peer], ret.at[i, row], bo_s.at[i, k], bo_r.at[i, k], row=peer),
            copy_to(bst.at[i, peer], rst.at[i, row], bs_s.at[i, k], bs_r.at[i, k], row=peer),
        )

    for i in range(1, n_col):
        send(q_copy(i))
    for k in range(1, n_row):
        branch_query(0, k).start()

    def flip(bit):
        return row + bit - 2 * bit * ((row // bit) % 2)

    mate, beside, below = flip(1), flip(2), flip(4)
    mate_copy = send(copy_to(root_ref, rootb.at[1], root_s.at[0], root_r.at[0], row=mate))
    rootb[0] = root_ref[...]

    first = 2 * (col % 2)

    def suffix_copy(h):
        return copy_to(suf_ref.at[:, pl.ds(h * HEAD_DIM, HEAD_DIM)], sbuf.at[col // 2], suf_s.at[h],
                       suf_r.at[col // 2], col=first + h)

    len_col = to_column(leaf_len_ref[...].astype(jnp.float32))
    key_at = lax.broadcasted_iota(jnp.int32, (1, leaf_keys), 1)
    key_leaf = (key_at // leaf_width).astype(jnp.float32)
    key_place = (col * leaf_width + key_at % leaf_width).astype(jnp.float32)
    rows32 = lax.broadcasted_iota(jnp.int32, (LEAF_ROW, leaf_keys), 0).astype(jnp.float32)
    key_len = jnp.sum(jnp.where(rows32 == key_leaf, len_col, 0.0), axis=0, keepdims=True)
    key_leaf = jnp.where(key_place < key_len, key_leaf, -1.0)
    leaf_col2 = jnp.concatenate([leaf_col, leaf_col], axis=0)

    loads[0].wait()
    loads[1].wait()

    def leaf_level(i):
        rows = stacked(qg[i])
        lm[i], ll[i], lo[i] = state_of(
            rows,
            lambda at, span: leafv[at:at + span, head_lanes(i)],
            lambda at, span: leafv[at:at + span, value_lanes(i)],
            lambda at, span: leaf_col2 == key_leaf[:, at:at + span],
            leaf_keys, held,
        )

    def arrive(i):
        q_copy(i).wait_recv()
        spread_out(i, qg[i])
        for k in range(1, n_row):
            branch_query(i, k).start()

    def leaf_and_next(i, carry):
        leaf_level(i)
        arrive(i + 1)
        return carry

    lax.fori_loop(0, n_col - 1, leaf_and_next, 0)
    beside_copy = send(copy_to(root_ref, rootb.at[2], root_s.at[1], root_r.at[1], row=beside))
    below_copy = send(copy_to(root_ref, rootb.at[4], root_s.at[2], root_r.at[2], row=below))
    for h in range(2):
        @pl.when(first + h != col)
        def _():
            suffix_copy(h).start()

        @pl.when(first + h == col)
        def _():
            sbuf[col // 2] = suf_ref[:, h * HEAD_DIM:(h + 1) * HEAD_DIM]

    leaf_level(n_col - 1)
    for i in range(n_col):
        brq[i, row] = sendq[i, row]

    loads[2].wait()
    loads[3].wait()
    slot_at = lax.broadcasted_iota(jnp.int32, (n_row, cap, 128), 1)
    lane_at = lax.broadcasted_iota(jnp.int32, (n_row, cap, 128), 2)

    def branch_level(i, carry):
        for k in range(1, n_row):
            branch_query(i, k).wait_recv()
        rows = stacked(brq[i].reshape(slots, PAIR))

        def usable(at, span):
            place = col * branch_keys + at + lax.broadcasted_iota(jnp.int32, (1, span), 1)
            return place < branch_len_ref[...]

        highest, totals, summed = state_of(
            rows,
            lambda at, span: branchv[at:at + span, head_lanes(i)],
            lambda at, span: branchv[at:at + span, value_lanes(i)],
            usable, branch_keys, held,
        )
        for j in range(2):
            for at, column in ((j, highest), (2 + j, totals)):
                column = jnp.broadcast_to(column[j * slots:(j + 1) * slots], (slots, 128))
                line = jnp.sum(
                    jnp.where(slot_at == lane_at, column.reshape(n_row, cap, 128), 0.0), axis=1, keepdims=True
                )
                bst[i, :, at:at + 1, :] = line
                bst[i, :, at + 4:at + 5, :] = line
        summed = jnp.concatenate([summed[:slots], summed[slots:]], axis=1).astype(jnp.bfloat16)
        bro[i] = summed.reshape(n_row, cap, PAIR)
        for k in range(1, n_row):
            for copy in branch_out(i, k):
                copy.start()
        return carry

    lax.fori_loop(0, n_col - 1, branch_level, 0)

    half = root_ref.shape[0] // 2
    beside_copy.wait_recv()
    below_copy.wait_recv()
    low_copy = send(copy_to(rootb.at[2, pl.ds(0, half)], rootb.at[6, pl.ds(0, half)], fwd_s.at[0],
                            fwd_r.at[0], row=below))
    high_copy = send(copy_to(rootb.at[4, pl.ds(half, half)], rootb.at[6, pl.ds(half, half)], fwd_s.at[1],
                             fwd_r.at[1], row=beside))
    shared = [
        send(copy_to(rootb.at[2], rootb.at[3], fwd_s.at[2], fwd_r.at[2], row=mate)),
        send(copy_to(rootb.at[4], rootb.at[5], fwd_s.at[3], fwd_r.at[3], row=mate)),
    ]
    branch_level(n_col - 1, 0)
    for i in range(n_col):
        ret[i, row] = bro[i, row]
        rst[i, row] = bst[i, row]

    mate_copy.wait_recv()
    for copy in shared:
        copy.wait_recv()

    def root_level(i, blocks):
        size = root_ref.shape[0]

        def part(lanes):
            def take(at, span):
                chosen = slice(blocks.start + at // size, blocks.start + (at + span) // size)
                return rootb[chosen, :, lanes].reshape(span, HEAD_DIM)
            return take

        state = state_of(
            stacked(qg[i]), part(head_lanes(i)), part(value_lanes(i)), None,
            (blocks.stop - blocks.start) * size, held,
        )
        lm[i], ll[i], lo[i] = join((lm[i], ll[i], lo[i]), state)

    def near_root(i, carry):
        root_level(i, slice(0, 6))
        return carry

    lax.fori_loop(0, n_col, near_root, 0)
    low_copy.wait_recv()
    high_copy.wait_recv()
    last = send(copy_to(rootb.at[6], rootb.at[7], fwd_s.at[4], fwd_r.at[4], row=mate))

    for i, local in ((0, 0), (1, n_col - 1)):
        @pl.when(col != local)
        def _():
            copy_to(suf_ref.at[:, pl.ds(0, HEAD_DIM)], sbuf.at[i], suf_s.at[0], suf_r.at[i],
                    col=(col + 1) % n_col).wait_recv()
    mask = (leaf_col2 == leaf_row) & (
        lax.broadcasted_iota(jnp.int32, (2 * tokens, tokens), 1)
        <= lax.broadcasted_iota(jnp.int32, (2 * tokens, tokens), 0) % tokens
    )
    own_state = state_of(
        stacked(q_ref[...]), lambda at, span: sbuf[0], lambda at, span: sbuf[1], lambda at, span: mask,
        tokens, held,
    )
    lm[0], ll[0], lo[0] = join((lm[0], ll[0], lo[0]), own_state)

    last.wait_recv()
    collect = jnp.where(
        lax.broadcasted_iota(jnp.int32, (tokens, slots), 1).astype(jnp.float32) == node_col * cap + rank_col,
        1.0, 0.0,
    ).astype(jnp.bfloat16)
    rank_here = along.astype(jnp.float32) == rank_col

    def final_copies(i):
        return (
            copy_to(fo.at[i], fin.at[i], f_s.at[i], f_r.at[i], col=group(i)),
            copy_to(fs.at[i], fins.at[i], fs_s.at[i], fs_r.at[i], col=group(i)),
        )

    def come_back(step, carry):
        i = (step + 1) % n_col
        root_level(i, slice(6, 8))
        for k in range(1, n_row):
            for copy in branch_out(i, k):
                copy.wait_recv()
        back = dot(collect, ret[i].reshape(slots, PAIR))
        stats = rst[i]

        def pick(index):
            found = jnp.zeros((tokens, 128), jnp.float32)
            for n in range(n_row):
                found = jnp.where(node_col == n, stats[n, index:index + 1, :], found)
            return jnp.sum(jnp.where(rank_here, found, 0.0), axis=1, keepdims=True)

        summed, lines = [], []
        for j in range(2):
            part = slice(j * tokens, (j + 1) * tokens)
            state = join(
                (lm[i, part], ll[i, part], lo[i, part]),
                (pick(j), pick(2 + j), back[:, j * HEAD_DIM:(j + 1) * HEAD_DIM]),
            )
            summed.append(state[2])
            lines += [to_row(state[0]), to_row(state[1])]
        fo[i] = jnp.concatenate(summed, axis=1).astype(jnp.bfloat16)
        fs[i] = jnp.concatenate(lines + lines, axis=0)

        @pl.when(i > 0)
        def _():
            for copy in final_copies(i):
                copy.start()

        return carry

    lax.fori_loop(0, n_col, come_back, 0)
    fin[0] = fo[0]
    fins[0] = fs[0]
    for i in range(1, n_col):
        for copy in final_copies(i):
            copy.wait_recv()
    for j in range(2):
        mine = None
        for i in range(n_col):
            lines = fins[i]
            other = (
                to_column(lines[2 * j:2 * j + 1]), to_column(lines[2 * j + 1:2 * j + 2]),
                fin[i, :, j * HEAD_DIM:(j + 1) * HEAD_DIM].astype(jnp.float32),
            )
            mine = other if mine is None else join(mine, other)
        out_ref[:, j * HEAD_DIM:(j + 1) * HEAD_DIM] = (mine[2] / mine[1]).astype(out_ref.dtype)

    for copy in sent:
        copy.wait_send()
    for h in range(2):
        @pl.when(first + h != col)
        def _():
            suffix_copy(h).wait_send()

    def drain(i, carry):
        for k in range(1, n_row):
            branch_query(i, k).wait_send()
            for copy in branch_out(i, k):
                copy.wait_send()

        @pl.when(i > 0)
        def _():
            for copy in final_copies(i):
                copy.wait_send()

        return carry

    lax.fori_loop(0, n_col, drain, 0)


def on_device_fused(
    queries, suffix_cache, suffix_leaf, leaf_parent, root_cache, branch_cache, branch_length, leaf_cache,
    leaf_length,
):
    n_row, n_col = lax.axis_size("row"), lax.axis_size("col")
    tokens = queries.shape[0]
    cap = tokens // 16 * (LEAF_ROW // n_row)
    slots = n_row * cap
    width = branch_cache.shape[2]
    branch = branch_cache.reshape(-1, width)
    leaf = leaf_cache.reshape(-1, width)
    bf16, f32 = jnp.bfloat16, jnp.float32
    dma = pltpu.SemaphoreType.DMA
    vmem = pltpu.VMEM
    scratch = [
        vmem((n_col, tokens, PAIR), bf16),
        vmem((2, tokens, HEAD_DIM), bf16),
        vmem((n_row,) + root_cache.shape, bf16),
        vmem(leaf.shape, bf16),
        vmem(branch.shape, bf16),
        vmem((n_col, n_row, cap, PAIR), bf16),
        vmem((n_col, n_row, cap, PAIR), bf16),
        vmem((n_col, n_row, cap, PAIR), bf16),
        vmem((n_col, n_row, 8, 128), f32),
        vmem((n_col, n_row, cap, PAIR), bf16),
        vmem((n_col, n_row, 8, 128), f32),
        vmem((KV_HEADS, 2 * tokens, 1), f32),
        vmem((KV_HEADS, 2 * tokens, 1), f32),
        vmem((KV_HEADS, 2 * tokens, HEAD_DIM), f32),
        vmem((KV_HEADS, tokens, PAIR), bf16),
        vmem((KV_HEADS, 8, tokens), f32),
        vmem((n_col, tokens, PAIR), bf16),
        vmem((n_col, 8, tokens), f32),
        vmem((max(2 * slots, 2 * tokens), max(branch.shape[0], leaf.shape[0])), f32),
        dma((4,)),
        dma((n_col,)), dma((n_col,)),
        dma((2,)), dma((2,)),
        dma((3,)), dma((3,)),
        dma((5,)), dma((5,)),
        dma((n_col, n_row)), dma((n_col, n_row)),
        dma((n_col, n_row)), dma((n_col, n_row)),
        dma((n_col, n_row)), dma((n_col, n_row)),
        dma((n_col,)), dma((n_col,)),
        dma((n_col,)), dma((n_col,)),
    ]
    in_vmem = pl.BlockSpec(memory_space=pltpu.VMEM)
    anywhere = pl.BlockSpec(memory_space=pl.ANY)
    return pl.pallas_call(
        functools.partial(fused_kernel, n_row, n_col, cap),
        out_shape=jax.ShapeDtypeStruct(queries.shape, queries.dtype),
        in_specs=[in_vmem] * 7 + [anywhere] * 2,
        out_specs=in_vmem,
        scratch_shapes=scratch,
        compiler_params=pltpu.CompilerParams(
            collective_id=0, has_side_effects=True, vmem_limit_bytes=56 * 2**20
        ),
    )(
        queries, suffix_cache, suffix_leaf, leaf_parent, leaf_length.reshape(1, -1),
        branch_length.reshape(1, 1), root_cache, branch, leaf,
    )


def solution(mesh):
    in_specs = (
        P("row", "col"),
        P("row", "col"),
        P("row", None),
        P("row", None),
        P(("row", "col"), None),
        P("row", "col", None),
        P("row"),
        P("row", "col", None),
        P("row"),
    )
    out_specs = P("row", "col")
    sizes = dict(mesh.shape)
    body = on_device_fused if (sizes["row"], sizes["col"]) == (8, 4) else on_device
    return jax.shard_map(
        body, mesh=mesh, in_specs=in_specs, out_specs=out_specs, check_vma=False
    )
```

```python
import functools
import math

import jax
import jax.numpy as jnp
from jax import lax
from jax.experimental import pallas as pl
from jax.experimental.pallas import tpu as pltpu
from jax.sharding import PartitionSpec as P

HEADS = 8
KV_HEADS = 4
HEAD_DIM = 256
LEAF_ROW = 32


NEG = -1e30


def attend(queries, keys_values, usable):
    row_count = queries.shape[0]
    key_count = keys_values.shape[0]
    group_size = HEADS // KV_HEADS
    key_width = KV_HEADS * HEAD_DIM
    query_heads = queries.reshape(row_count, KV_HEADS, group_size, HEAD_DIM)
    key_heads = keys_values[:, :key_width].reshape(key_count, KV_HEADS, HEAD_DIM)
    value_heads = keys_values[:, key_width:].reshape(key_count, KV_HEADS, HEAD_DIM)
    scores = jnp.einsum(
        "rgjd,kgd->rgjk", query_heads, key_heads, preferred_element_type=jnp.float32
    ) * (1.0 / math.sqrt(HEAD_DIM))
    if usable is not None:
        key_mask = usable[:, None, None, :]
        scores = jnp.where(key_mask, scores, NEG)
    highest = jnp.max(scores, axis=-1)
    weights = jnp.exp(scores - highest[..., None])
    if usable is not None:
        weights = jnp.where(key_mask, weights, 0.0)
    totals = jnp.sum(weights, axis=-1)
    summed = jnp.einsum(
        "rgjk,kgd->rgjd",
        weights.astype(jnp.bfloat16),
        value_heads,
        preferred_element_type=jnp.float32,
    )
    return (
        highest.reshape(row_count, HEADS),
        totals.reshape(row_count, HEADS),
        summed.reshape(row_count, HEADS * HEAD_DIM),
    )


def merge_state(earlier, others):
    highest = jnp.maximum(earlier[0], others[0])
    keep_first = jnp.exp(earlier[0] - highest)
    keep_second = jnp.exp(others[0] - highest)
    totals = earlier[1] * keep_first + others[1] * keep_second
    summed = earlier[2] * jnp.repeat(keep_first, HEAD_DIM, axis=1) + others[2] * jnp.repeat(
        keep_second, HEAD_DIM, axis=1
    )
    return (highest, totals, summed)


def slice_heads(values, col_index, feature_width):
    per_slice = max(1, feature_width // HEAD_DIM)
    first_head = col_index * feature_width // HEAD_DIM
    chosen = lax.dynamic_slice_in_dim(values, first_head, per_slice, values.ndim - 1)
    return jnp.repeat(chosen, feature_width // per_slice, axis=values.ndim - 1)


def combine_columns(running):
    highest, totals, summed = running
    overall = lax.pmax(highest, "col")
    factors = jnp.exp(highest - overall)
    slice_sum = lax.psum_scatter(
        summed * jnp.repeat(factors, HEAD_DIM, axis=1), "col", scatter_dimension=1, tiled=True
    )
    overall_total = lax.psum(totals * factors, "col")
    return (overall, overall_total, slice_sum)


def on_device(
    queries,
    suffix_cache,
    suffix_leaf,
    leaf_parent,
    root_cache,
    branch_cache,
    branch_length,
    leaf_cache,
    leaf_length,
):
    col_count = lax.axis_size("col")
    row_count = lax.axis_size("row")
    col_index = lax.axis_index("col")
    full_queries, full_suffix = (
        lax.all_gather(queries, "col", axis=1, tiled=True),
        lax.all_gather(suffix_cache, "col", axis=1, tiled=True),
    )
    token_count = full_queries.shape[0]
    query_width = full_queries.shape[1]
    feature_width = queries.shape[1]
    leaf_local = suffix_leaf[0]
    positions = jnp.arange(token_count, dtype=jnp.int32)
    blank_state = (
        jnp.full((token_count, HEADS), NEG, jnp.float32),
        jnp.zeros((token_count, HEADS), jnp.float32),
        jnp.zeros((token_count, query_width), jnp.float32),
    )
    running = merge_state(
        blank_state,
        attend(full_queries, lax.all_gather(root_cache, "row", axis=0, tiled=True), None),
    )
    leaf_width = leaf_cache.shape[1]
    leaf_keys = leaf_cache.reshape(LEAF_ROW * leaf_width, leaf_cache.shape[2])
    key_slot = jnp.arange(LEAF_ROW * leaf_width, dtype=jnp.int32)
    key_leaf = key_slot // leaf_width
    key_place = col_index * leaf_width + key_slot % leaf_width
    leaf_ids = jnp.arange(LEAF_ROW, dtype=jnp.int32)
    key_live = jnp.any(
        (key_leaf[None, :] == leaf_ids[:, None]) & (key_place[None, :] < leaf_length[:, None]),
        axis=0,
    )
    usable = (leaf_local[:, None] == key_leaf[None, :]) & key_live[None, :]
    running = merge_state(running, attend(full_queries, leaf_keys, usable))
    suffix_width = token_count // col_count
    suffix_start = col_index * suffix_width
    suffix_keys = lax.dynamic_slice_in_dim(full_suffix, suffix_start, suffix_width, 0)
    suffix_owner = lax.dynamic_slice_in_dim(leaf_local, suffix_start, suffix_width, 0)
    suffix_place = suffix_start + jnp.arange(suffix_width, dtype=jnp.int32)
    usable = (leaf_local[:, None] == suffix_owner[None, :]) & (
        suffix_place[None, :] <= positions[:, None]
    )
    running = merge_state(running, attend(full_queries, suffix_keys, usable))
    parents = leaf_parent[0]
    token_node = jnp.sum(
        jnp.where(leaf_local[:, None] == leaf_ids[None, :], parents[None, :], 0), axis=1
    )
    node_ids = jnp.arange(row_count, dtype=jnp.int32)
    node_hits = (token_node[:, None] == node_ids[None, :]).astype(jnp.int32)
    rank_in_node = jnp.sum(node_hits * (jnp.cumsum(node_hits, axis=0) - 1), axis=1)
    capacity = token_count // 16 * (LEAF_ROW // row_count)
    slot_index = token_node * capacity + rank_in_node
    slot_token = (
        jnp.full((row_count * capacity,), token_count, jnp.int32).at[slot_index].set(positions)
    )
    padded = jnp.concatenate(
        [full_queries, jnp.zeros((1, query_width), full_queries.dtype)], axis=0
    )
    outgoing = padded[slot_token].reshape(row_count, capacity, query_width)
    branch_keys = branch_cache[0]
    branch_width = branch_keys.shape[0]
    branch_place = col_index * branch_width + jnp.arange(branch_width, dtype=jnp.int32)
    branch_usable = (branch_place < branch_length[0])[None, :]
    arrived = lax.all_to_all(outgoing, "row", split_axis=0, concat_axis=0, tiled=True)
    sources = arrived.shape[0]
    item_count = arrived.shape[1]
    flat_queries = arrived.reshape(sources * item_count, arrived.shape[2])
    highest, totals, summed = attend(flat_queries, branch_keys, branch_usable)
    returned = (
        lax.all_to_all(
            summed.reshape(sources, item_count, query_width),
            "row",
            split_axis=0,
            concat_axis=0,
            tiled=True,
        ),
        lax.all_to_all(
            highest.reshape(sources, item_count, HEADS),
            "row",
            split_axis=0,
            concat_axis=0,
            tiled=True,
        ),
        lax.all_to_all(
            totals.reshape(sources, item_count, HEADS),
            "row",
            split_axis=0,
            concat_axis=0,
            tiled=True,
        ),
    )
    back_sums = returned[0].reshape(row_count * capacity, returned[0].shape[2])[slot_index]
    back_peaks = returned[1].reshape(row_count * capacity, HEADS)[slot_index]
    back_totals = returned[2].reshape(row_count * capacity, HEADS)[slot_index]
    running = merge_state(running, (back_peaks, back_totals, back_sums))
    highest, totals, summed = combine_columns(running)
    output = summed / slice_heads(totals, col_index, feature_width)
    return output.astype(jnp.bfloat16)


LOW = -1e28
LOG2_SCALE = 1.0 / (math.sqrt(HEAD_DIM) * math.log(2.0))
KEY_WIDTH = KV_HEADS * HEAD_DIM
PAIR = HEADS // KV_HEADS * HEAD_DIM
KEY_STEP = 256
VALUE_STEP = 512
NT = (((1,), (1,)), ((), ()))
NN = (((1,), (0,)), ((), ()))


def dot(a, b, dims=NN, precision=None):
    return lax.dot_general(a, b, dims, precision=precision, preferred_element_type=jnp.float32)


def fold_lanes(values, operation):
    folded = values[:, :128]
    for at in range(128, values.shape[1], 128):
        folded = operation(folded, values[:, at:at + 128])
    return folded


def state_of(query_rows, keys, values, mask, count, held):
    rows = query_rows.shape[0]
    widest = None
    for at in range(0, count, KEY_STEP):
        span = min(KEY_STEP, count - at)
        scores = dot(query_rows, keys(at, span), NT)
        if mask is not None:
            scores = jnp.where(mask(at, span), scores, NEG)
        held[:rows, at:at + span] = scores
        folded = fold_lanes(scores, jnp.maximum)
        widest = folded if widest is None else jnp.maximum(widest, folded)
    highest = jnp.maximum(jnp.max(widest, axis=1, keepdims=True) * LOG2_SCALE, LOW)
    totals, summed = None, None
    for at in range(0, count, VALUE_STEP):
        span = min(VALUE_STEP, count - at)
        weights = jnp.exp2(held[:rows, at:at + span] * LOG2_SCALE - highest)
        folded = fold_lanes(weights, jnp.add)
        totals = folded if totals is None else totals + folded
        product = dot(weights.astype(jnp.bfloat16), values(at, span))
        summed = product if summed is None else summed + product
    return highest, jnp.sum(totals, axis=1, keepdims=True), summed


def join(first, second):
    highest = jnp.maximum(first[0], second[0])
    a, b = jnp.exp2(first[0] - highest), jnp.exp2(second[0] - highest)
    return highest, first[1] * a + second[1] * b, first[2] * a + second[2] * b


def stacked(pair):
    return jnp.concatenate([pair[:, :HEAD_DIM], pair[:, HEAD_DIM:]], axis=0)


def fused_kernel(
    n_row, n_col, cap,
    q_ref, suf_ref, leaf_of_ref, parent_ref, leaf_len_ref, branch_len_ref, root_ref, branch_ref, leaf_ref,
    out_ref,
    qg, sbuf, rootb, leafv, branchv, sendq, brq, bro, bst, ret, rst, lm, ll, lo, fo, fs, fin, fins, held,
    load_sem, q_s, q_r, suf_s, suf_r, root_s, root_r, fwd_s, fwd_r, bq_s, bq_r, bo_s, bo_r, bs_s, bs_r,
    f_s, f_r, fs_s, fs_r,
):
    row, col = lax.axis_index("row"), lax.axis_index("col")
    tokens = q_ref.shape[0]
    slots = n_row * cap
    branch_keys, leaf_keys = branchv.shape[0], leafv.shape[0]
    leaf_width = leaf_keys // LEAF_ROW

    def copy_to(src, dst, s, r, **where):
        return pltpu.make_async_remote_copy(
            src_ref=src, dst_ref=dst, send_sem=s, recv_sem=r, device_id=where,
            device_id_type=pl.DeviceIdType.MESH,
        )

    def group(i):
        return (col + i) % 2 + 2 * ((col // 2 + i // 2) % 2)

    def head_lanes(i):
        return pl.ds(pl.multiple_of(group(i) * HEAD_DIM, HEAD_DIM), HEAD_DIM)

    def value_lanes(i):
        return pl.ds(pl.multiple_of(KEY_WIDTH + group(i) * HEAD_DIM, HEAD_DIM), HEAD_DIM)

    loads = []
    for i, (src, dst) in enumerate(((leaf_ref, leafv), (branch_ref, branchv))):
        step = dst.shape[0] // 2
        for j in range(2):
            part = pl.ds(j * step, step)
            loads.append(pltpu.make_async_copy(src.at[part], dst.at[part], load_sem.at[2 * i + j]))
    for load in loads:
        load.start()

    barrier = pltpu.get_barrier_semaphore()
    for k in range(1, n_row):
        pl.semaphore_signal(barrier, inc=1, device_id={"row": (row + k) % n_row},
                            device_id_type=pl.DeviceIdType.MESH)
    for k in range(1, n_col):
        pl.semaphore_signal(barrier, inc=1, device_id={"col": (col + k) % n_col},
                            device_id_type=pl.DeviceIdType.MESH)

    def eye(n):
        return lax.broadcasted_iota(jnp.int32, (n, n), 0) == lax.broadcasted_iota(jnp.int32, (n, n), 1)

    def to_column(values):
        return jnp.sum(jnp.where(eye(values.shape[1]), values, 0.0), axis=1, keepdims=True)

    def to_row(values):
        return jnp.sum(jnp.where(eye(values.shape[0]), values, 0.0), axis=0, keepdims=True)

    leaf_row = leaf_of_ref[...].astype(jnp.float32)
    leaf_col = to_column(leaf_row)
    parent_row = parent_ref[...].astype(jnp.float32)
    leaf_iota = lax.broadcasted_iota(jnp.int32, (tokens, LEAF_ROW), 1).astype(jnp.float32)
    node_col = jnp.sum(jnp.where(leaf_col == leaf_iota, parent_row, 0.0), axis=1, keepdims=True)
    node_row = to_row(node_col)
    above = lax.broadcasted_iota(jnp.int32, (tokens, tokens), 0)
    along = lax.broadcasted_iota(jnp.int32, (tokens, tokens), 1)
    earlier = jnp.where((node_col == node_row) & (along < above), 1.0, 0.0)
    rank_col = jnp.sum(earlier, axis=1, keepdims=True)
    slot_row = to_row(node_col * cap + rank_col)
    spread = jnp.where(
        lax.broadcasted_iota(jnp.int32, (slots, tokens), 0).astype(jnp.float32) == slot_row, 1.0, 0.0
    ).astype(jnp.bfloat16)

    def spread_out(i, pair):
        sendq[i] = dot(spread, pair).astype(jnp.bfloat16).reshape(n_row, cap, PAIR)

    qg[0] = q_ref[...]
    spread_out(0, q_ref[...])
    pl.semaphore_wait(barrier, n_row + n_col - 2)

    sent = []

    def send(copy):
        copy.start()
        sent.append(copy)
        return copy

    def q_copy(i):
        return copy_to(q_ref, qg.at[i], q_s.at[i], q_r.at[i], col=group(i))

    def branch_query(i, k):
        peer = (row + k) % n_row
        return copy_to(sendq.at[i, peer], brq.at[i, row], bq_s.at[i, k], bq_r.at[i, k], row=peer)

    def branch_out(i, k):
        peer = (row + k) % n_row
        return (
            copy_to(bro.at[i, peer], ret.at[i, row], bo_s.at[i, k], bo_r.at[i, k], row=peer),
            copy_to(bst.at[i, peer], rst.at[i, row], bs_s.at[i, k], bs_r.at[i, k], row=peer),
        )

    for i in range(1, n_col):
        send(q_copy(i))
    for k in range(1, n_row):
        branch_query(0, k).start()

    def flip(bit):
        return row + bit - 2 * bit * ((row // bit) % 2)

    mate, beside, below = flip(1), flip(2), flip(4)
    mate_copy = send(copy_to(root_ref, rootb.at[1], root_s.at[0], root_r.at[0], row=mate))
    beside_copy = send(copy_to(root_ref, rootb.at[2], root_s.at[1], root_r.at[1], row=beside))
    below_copy = send(copy_to(root_ref, rootb.at[4], root_s.at[2], root_r.at[2], row=below))
    rootb[0] = root_ref[...]

    first = 2 * (col % 2)

    def suffix_copy(h):
        return copy_to(suf_ref.at[:, pl.ds(h * HEAD_DIM, HEAD_DIM)], sbuf.at[col // 2], suf_s.at[h],
                       suf_r.at[col // 2], col=first + h)

    len_col = to_column(leaf_len_ref[...].astype(jnp.float32))
    key_at = lax.broadcasted_iota(jnp.int32, (1, leaf_keys), 1)
    key_leaf = (key_at // leaf_width).astype(jnp.float32)
    key_place = (col * leaf_width + key_at % leaf_width).astype(jnp.float32)
    rows32 = lax.broadcasted_iota(jnp.int32, (LEAF_ROW, leaf_keys), 0).astype(jnp.float32)
    key_len = jnp.sum(jnp.where(rows32 == key_leaf, len_col, 0.0), axis=0, keepdims=True)
    key_leaf = jnp.where(key_place < key_len, key_leaf, -1.0)
    leaf_col2 = jnp.concatenate([leaf_col, leaf_col], axis=0)

    loads[0].wait()
    loads[1].wait()

    def leaf_level(i):
        rows = stacked(qg[i])
        lm[i], ll[i], lo[i] = state_of(
            rows,
            lambda at, span: leafv[at:at + span, head_lanes(i)],
            lambda at, span: leafv[at:at + span, value_lanes(i)],
            lambda at, span: leaf_col2 == key_leaf[:, at:at + span],
            leaf_keys, held,
        )

    def arrive(i):
        q_copy(i).wait_recv()
        spread_out(i, qg[i])
        for k in range(1, n_row):
            branch_query(i, k).start()

    def leaf_and_next(i, carry):
        leaf_level(i)
        arrive(i + 1)
        return carry

    lax.fori_loop(0, n_col - 1, leaf_and_next, 0)
    half = root_ref.shape[0] // 2
    beside_copy.wait_recv()
    below_copy.wait_recv()
    low_copy = send(copy_to(rootb.at[2, pl.ds(0, half)], rootb.at[6, pl.ds(0, half)], fwd_s.at[0],
                            fwd_r.at[0], row=below))
    high_copy = send(copy_to(rootb.at[4, pl.ds(half, half)], rootb.at[6, pl.ds(half, half)], fwd_s.at[1],
                             fwd_r.at[1], row=beside))
    shared = [
        send(copy_to(rootb.at[2], rootb.at[3], fwd_s.at[2], fwd_r.at[2], row=mate)),
        send(copy_to(rootb.at[4], rootb.at[5], fwd_s.at[3], fwd_r.at[3], row=mate)),
    ]
    for h in range(2):
        @pl.when(first + h != col)
        def _():
            suffix_copy(h).start()

        @pl.when(first + h == col)
        def _():
            sbuf[col // 2] = suf_ref[:, h * HEAD_DIM:(h + 1) * HEAD_DIM]

    leaf_level(n_col - 1)
    for i in range(n_col):
        brq[i, row] = sendq[i, row]

    loads[2].wait()
    loads[3].wait()
    slot_at = lax.broadcasted_iota(jnp.int32, (n_row, cap, 128), 1)
    lane_at = lax.broadcasted_iota(jnp.int32, (n_row, cap, 128), 2)

    def branch_level(i, carry):
        for k in range(1, n_row):
            branch_query(i, k).wait_recv()
        rows = stacked(brq[i].reshape(slots, PAIR))

        def usable(at, span):
            place = col * branch_keys + at + lax.broadcasted_iota(jnp.int32, (1, span), 1)
            return place < branch_len_ref[...]

        highest, totals, summed = state_of(
            rows,
            lambda at, span: branchv[at:at + span, head_lanes(i)],
            lambda at, span: branchv[at:at + span, value_lanes(i)],
            usable, branch_keys, held,
        )
        for j in range(2):
            for at, column in ((j, highest), (2 + j, totals)):
                column = jnp.broadcast_to(column[j * slots:(j + 1) * slots], (slots, 128))
                line = jnp.sum(
                    jnp.where(slot_at == lane_at, column.reshape(n_row, cap, 128), 0.0), axis=1, keepdims=True
                )
                bst[i, :, at:at + 1, :] = line
                bst[i, :, at + 4:at + 5, :] = line
        summed = jnp.concatenate([summed[:slots], summed[slots:]], axis=1).astype(jnp.bfloat16)
        bro[i] = summed.reshape(n_row, cap, PAIR)
        for k in range(1, n_row):
            for copy in branch_out(i, k):
                copy.start()
        return carry

    lax.fori_loop(0, n_col - 1, branch_level, 0)

    low_copy.wait_recv()
    high_copy.wait_recv()
    last = send(copy_to(rootb.at[6], rootb.at[7], fwd_s.at[4], fwd_r.at[4], row=mate))
    branch_level(n_col - 1, 0)
    for i in range(n_col):
        ret[i, row] = bro[i, row]
        rst[i, row] = bst[i, row]

    mate_copy.wait_recv()
    for copy in shared:
        copy.wait_recv()
    last.wait_recv()

    def root_level(i, blocks):
        size = root_ref.shape[0]

        def part(lanes):
            def take(at, span):
                chosen = slice(blocks.start + at // size, blocks.start + (at + span) // size)
                return rootb[chosen, :, lanes].reshape(span, HEAD_DIM)
            return take

        state = state_of(
            stacked(qg[i]), part(head_lanes(i)), part(value_lanes(i)), None,
            (blocks.stop - blocks.start) * size, held,
        )
        lm[i], ll[i], lo[i] = join((lm[i], ll[i], lo[i]), state)

    def all_root(i, carry):
        root_level(i, slice(0, n_row))
        return carry

    lax.fori_loop(0, n_col, all_root, 0)

    for i, local in ((0, 0), (1, n_col - 1)):
        @pl.when(col != local)
        def _():
            copy_to(suf_ref.at[:, pl.ds(0, HEAD_DIM)], sbuf.at[i], suf_s.at[0], suf_r.at[i],
                    col=(col + 1) % n_col).wait_recv()
    mask = (leaf_col2 == leaf_row) & (
        lax.broadcasted_iota(jnp.int32, (2 * tokens, tokens), 1)
        <= lax.broadcasted_iota(jnp.int32, (2 * tokens, tokens), 0) % tokens
    )
    own_state = state_of(
        stacked(q_ref[...]), lambda at, span: sbuf[0], lambda at, span: sbuf[1], lambda at, span: mask,
        tokens, held,
    )
    lm[0], ll[0], lo[0] = join((lm[0], ll[0], lo[0]), own_state)

    collect = jnp.where(
        lax.broadcasted_iota(jnp.int32, (tokens, slots), 1).astype(jnp.float32) == node_col * cap + rank_col,
        1.0, 0.0,
    ).astype(jnp.bfloat16)
    rank_here = along.astype(jnp.float32) == rank_col

    def final_copies(i):
        return (
            copy_to(fo.at[i], fin.at[i], f_s.at[i], f_r.at[i], col=group(i)),
            copy_to(fs.at[i], fins.at[i], fs_s.at[i], fs_r.at[i], col=group(i)),
        )

    def come_back(step, carry):
        i = (step + 1) % n_col
        for k in range(1, n_row):
            for copy in branch_out(i, k):
                copy.wait_recv()
        back = dot(collect, ret[i].reshape(slots, PAIR))
        stats = rst[i]

        def pick(index):
            found = jnp.zeros((tokens, 128), jnp.float32)
            for n in range(n_row):
                found = jnp.where(node_col == n, stats[n, index:index + 1, :], found)
            return jnp.sum(jnp.where(rank_here, found, 0.0), axis=1, keepdims=True)

        summed, lines = [], []
        for j in range(2):
            part = slice(j * tokens, (j + 1) * tokens)
            state = join(
                (lm[i, part], ll[i, part], lo[i, part]),
                (pick(j), pick(2 + j), back[:, j * HEAD_DIM:(j + 1) * HEAD_DIM]),
            )
            summed.append(state[2])
            lines += [to_row(state[0]), to_row(state[1])]
        fo[i] = jnp.concatenate(summed, axis=1).astype(jnp.bfloat16)
        fs[i] = jnp.concatenate(lines + lines, axis=0)

        @pl.when(i > 0)
        def _():
            for copy in final_copies(i):
                copy.start()

        return carry

    lax.fori_loop(0, n_col, come_back, 0)
    fin[0] = fo[0]
    fins[0] = fs[0]
    for i in range(1, n_col):
        for copy in final_copies(i):
            copy.wait_recv()
    for j in range(2):
        mine = None
        for i in range(n_col):
            lines = fins[i]
            other = (
                to_column(lines[2 * j:2 * j + 1]), to_column(lines[2 * j + 1:2 * j + 2]),
                fin[i, :, j * HEAD_DIM:(j + 1) * HEAD_DIM].astype(jnp.float32),
            )
            mine = other if mine is None else join(mine, other)
        out_ref[:, j * HEAD_DIM:(j + 1) * HEAD_DIM] = (mine[2] / mine[1]).astype(out_ref.dtype)

    for copy in sent:
        copy.wait_send()
    for h in range(2):
        @pl.when(first + h != col)
        def _():
            suffix_copy(h).wait_send()

    def drain(i, carry):
        for k in range(1, n_row):
            branch_query(i, k).wait_send()
            for copy in branch_out(i, k):
                copy.wait_send()

        @pl.when(i > 0)
        def _():
            for copy in final_copies(i):
                copy.wait_send()

        return carry

    lax.fori_loop(0, n_col, drain, 0)


def on_device_fused(
    queries, suffix_cache, suffix_leaf, leaf_parent, root_cache, branch_cache, branch_length, leaf_cache,
    leaf_length,
):
    n_row, n_col = lax.axis_size("row"), lax.axis_size("col")
    tokens = queries.shape[0]
    cap = tokens // 16 * (LEAF_ROW // n_row)
    slots = n_row * cap
    width = branch_cache.shape[2]
    branch = branch_cache.reshape(-1, width)
    leaf = leaf_cache.reshape(-1, width)
    bf16, f32 = jnp.bfloat16, jnp.float32
    dma = pltpu.SemaphoreType.DMA
    vmem = pltpu.VMEM
    scratch = [
        vmem((n_col, tokens, PAIR), bf16),
        vmem((2, tokens, HEAD_DIM), bf16),
        vmem((n_row,) + root_cache.shape, bf16),
        vmem(leaf.shape, bf16),
        vmem(branch.shape, bf16),
        vmem((n_col, n_row, cap, PAIR), bf16),
        vmem((n_col, n_row, cap, PAIR), bf16),
        vmem((n_col, n_row, cap, PAIR), bf16),
        vmem((n_col, n_row, 8, 128), f32),
        vmem((n_col, n_row, cap, PAIR), bf16),
        vmem((n_col, n_row, 8, 128), f32),
        vmem((KV_HEADS, 2 * tokens, 1), f32),
        vmem((KV_HEADS, 2 * tokens, 1), f32),
        vmem((KV_HEADS, 2 * tokens, HEAD_DIM), f32),
        vmem((KV_HEADS, tokens, PAIR), bf16),
        vmem((KV_HEADS, 8, tokens), f32),
        vmem((n_col, tokens, PAIR), bf16),
        vmem((n_col, 8, tokens), f32),
        vmem((max(2 * slots, 2 * tokens), max(branch.shape[0], leaf.shape[0])), f32),
        dma((4,)),
        dma((n_col,)), dma((n_col,)),
        dma((2,)), dma((2,)),
        dma((3,)), dma((3,)),
        dma((5,)), dma((5,)),
        dma((n_col, n_row)), dma((n_col, n_row)),
        dma((n_col, n_row)), dma((n_col, n_row)),
        dma((n_col, n_row)), dma((n_col, n_row)),
        dma((n_col,)), dma((n_col,)),
        dma((n_col,)), dma((n_col,)),
    ]
    in_vmem = pl.BlockSpec(memory_space=pltpu.VMEM)
    anywhere = pl.BlockSpec(memory_space=pl.ANY)
    return pl.pallas_call(
        functools.partial(fused_kernel, n_row, n_col, cap),
        out_shape=jax.ShapeDtypeStruct(queries.shape, queries.dtype),
        in_specs=[in_vmem] * 7 + [anywhere] * 2,
        out_specs=in_vmem,
        scratch_shapes=scratch,
        compiler_params=pltpu.CompilerParams(
            collective_id=0, has_side_effects=True, vmem_limit_bytes=56 * 2**20
        ),
    )(
        queries, suffix_cache, suffix_leaf, leaf_parent, leaf_length.reshape(1, -1),
        branch_length.reshape(1, 1), root_cache, branch, leaf,
    )


def solution(mesh):
    in_specs = (
        P("row", "col"),
        P("row", "col"),
        P("row", None),
        P("row", None),
        P(("row", "col"), None),
        P("row", "col", None),
        P("row"),
        P("row", "col", None),
        P("row"),
    )
    out_specs = P("row", "col")
    sizes = dict(mesh.shape)
    body = on_device_fused if (sizes["row"], sizes["col"]) == (8, 4) else on_device
    return jax.shard_map(
        body, mesh=mesh, in_specs=in_specs, out_specs=out_specs, check_vma=False
    )
```

```python
import functools
import math

import jax
import jax.numpy as jnp
from jax import lax
from jax.experimental import pallas as pl
from jax.experimental.pallas import tpu as pltpu
from jax.sharding import PartitionSpec as P

HEADS = 8
KV_HEADS = 4
HEAD_DIM = 256
LEAF_ROW = 32


NEG = -1e30


def attend(queries, keys_values, usable):
    row_count = queries.shape[0]
    key_count = keys_values.shape[0]
    group_size = HEADS // KV_HEADS
    key_width = KV_HEADS * HEAD_DIM
    query_heads = queries.reshape(row_count, KV_HEADS, group_size, HEAD_DIM)
    key_heads = keys_values[:, :key_width].reshape(key_count, KV_HEADS, HEAD_DIM)
    value_heads = keys_values[:, key_width:].reshape(key_count, KV_HEADS, HEAD_DIM)
    scores = jnp.einsum(
        "rgjd,kgd->rgjk", query_heads, key_heads, preferred_element_type=jnp.float32
    ) * (1.0 / math.sqrt(HEAD_DIM))
    if usable is not None:
        key_mask = usable[:, None, None, :]
        scores = jnp.where(key_mask, scores, NEG)
    highest = jnp.max(scores, axis=-1)
    weights = jnp.exp(scores - highest[..., None])
    if usable is not None:
        weights = jnp.where(key_mask, weights, 0.0)
    totals = jnp.sum(weights, axis=-1)
    summed = jnp.einsum(
        "rgjk,kgd->rgjd",
        weights.astype(jnp.bfloat16),
        value_heads,
        preferred_element_type=jnp.float32,
    )
    return (
        highest.reshape(row_count, HEADS),
        totals.reshape(row_count, HEADS),
        summed.reshape(row_count, HEADS * HEAD_DIM),
    )


def merge_state(earlier, others):
    highest = jnp.maximum(earlier[0], others[0])
    keep_first = jnp.exp(earlier[0] - highest)
    keep_second = jnp.exp(others[0] - highest)
    totals = earlier[1] * keep_first + others[1] * keep_second
    summed = earlier[2] * jnp.repeat(keep_first, HEAD_DIM, axis=1) + others[2] * jnp.repeat(
        keep_second, HEAD_DIM, axis=1
    )
    return (highest, totals, summed)


def slice_heads(values, col_index, feature_width):
    per_slice = max(1, feature_width // HEAD_DIM)
    first_head = col_index * feature_width // HEAD_DIM
    chosen = lax.dynamic_slice_in_dim(values, first_head, per_slice, values.ndim - 1)
    return jnp.repeat(chosen, feature_width // per_slice, axis=values.ndim - 1)


def combine_columns(running):
    highest, totals, summed = running
    overall = lax.pmax(highest, "col")
    factors = jnp.exp(highest - overall)
    slice_sum = lax.psum_scatter(
        summed * jnp.repeat(factors, HEAD_DIM, axis=1), "col", scatter_dimension=1, tiled=True
    )
    overall_total = lax.psum(totals * factors, "col")
    return (overall, overall_total, slice_sum)


def on_device(
    queries,
    suffix_cache,
    suffix_leaf,
    leaf_parent,
    root_cache,
    branch_cache,
    branch_length,
    leaf_cache,
    leaf_length,
):
    col_count = lax.axis_size("col")
    row_count = lax.axis_size("row")
    col_index = lax.axis_index("col")
    full_queries, full_suffix = (
        lax.all_gather(queries, "col", axis=1, tiled=True),
        lax.all_gather(suffix_cache, "col", axis=1, tiled=True),
    )
    token_count = full_queries.shape[0]
    query_width = full_queries.shape[1]
    feature_width = queries.shape[1]
    leaf_local = suffix_leaf[0]
    positions = jnp.arange(token_count, dtype=jnp.int32)
    blank_state = (
        jnp.full((token_count, HEADS), NEG, jnp.float32),
        jnp.zeros((token_count, HEADS), jnp.float32),
        jnp.zeros((token_count, query_width), jnp.float32),
    )
    running = merge_state(
        blank_state,
        attend(full_queries, lax.all_gather(root_cache, "row", axis=0, tiled=True), None),
    )
    leaf_width = leaf_cache.shape[1]
    leaf_keys = leaf_cache.reshape(LEAF_ROW * leaf_width, leaf_cache.shape[2])
    key_slot = jnp.arange(LEAF_ROW * leaf_width, dtype=jnp.int32)
    key_leaf = key_slot // leaf_width
    key_place = col_index * leaf_width + key_slot % leaf_width
    leaf_ids = jnp.arange(LEAF_ROW, dtype=jnp.int32)
    key_live = jnp.any(
        (key_leaf[None, :] == leaf_ids[:, None]) & (key_place[None, :] < leaf_length[:, None]),
        axis=0,
    )
    usable = (leaf_local[:, None] == key_leaf[None, :]) & key_live[None, :]
    running = merge_state(running, attend(full_queries, leaf_keys, usable))
    suffix_width = token_count // col_count
    suffix_start = col_index * suffix_width
    suffix_keys = lax.dynamic_slice_in_dim(full_suffix, suffix_start, suffix_width, 0)
    suffix_owner = lax.dynamic_slice_in_dim(leaf_local, suffix_start, suffix_width, 0)
    suffix_place = suffix_start + jnp.arange(suffix_width, dtype=jnp.int32)
    usable = (leaf_local[:, None] == suffix_owner[None, :]) & (
        suffix_place[None, :] <= positions[:, None]
    )
    running = merge_state(running, attend(full_queries, suffix_keys, usable))
    parents = leaf_parent[0]
    token_node = jnp.sum(
        jnp.where(leaf_local[:, None] == leaf_ids[None, :], parents[None, :], 0), axis=1
    )
    node_ids = jnp.arange(row_count, dtype=jnp.int32)
    node_hits = (token_node[:, None] == node_ids[None, :]).astype(jnp.int32)
    rank_in_node = jnp.sum(node_hits * (jnp.cumsum(node_hits, axis=0) - 1), axis=1)
    capacity = token_count // 16 * (LEAF_ROW // row_count)
    slot_index = token_node * capacity + rank_in_node
    slot_token = (
        jnp.full((row_count * capacity,), token_count, jnp.int32).at[slot_index].set(positions)
    )
    padded = jnp.concatenate(
        [full_queries, jnp.zeros((1, query_width), full_queries.dtype)], axis=0
    )
    outgoing = padded[slot_token].reshape(row_count, capacity, query_width)
    branch_keys = branch_cache[0]
    branch_width = branch_keys.shape[0]
    branch_place = col_index * branch_width + jnp.arange(branch_width, dtype=jnp.int32)
    branch_usable = (branch_place < branch_length[0])[None, :]
    arrived = lax.all_to_all(outgoing, "row", split_axis=0, concat_axis=0, tiled=True)
    sources = arrived.shape[0]
    item_count = arrived.shape[1]
    flat_queries = arrived.reshape(sources * item_count, arrived.shape[2])
    highest, totals, summed = attend(flat_queries, branch_keys, branch_usable)
    returned = (
        lax.all_to_all(
            summed.reshape(sources, item_count, query_width),
            "row",
            split_axis=0,
            concat_axis=0,
            tiled=True,
        ),
        lax.all_to_all(
            highest.reshape(sources, item_count, HEADS),
            "row",
            split_axis=0,
            concat_axis=0,
            tiled=True,
        ),
        lax.all_to_all(
            totals.reshape(sources, item_count, HEADS),
            "row",
            split_axis=0,
            concat_axis=0,
            tiled=True,
        ),
    )
    back_sums = returned[0].reshape(row_count * capacity, returned[0].shape[2])[slot_index]
    back_peaks = returned[1].reshape(row_count * capacity, HEADS)[slot_index]
    back_totals = returned[2].reshape(row_count * capacity, HEADS)[slot_index]
    running = merge_state(running, (back_peaks, back_totals, back_sums))
    highest, totals, summed = combine_columns(running)
    output = summed / slice_heads(totals, col_index, feature_width)
    return output.astype(jnp.bfloat16)


LOW = -1e28
LOG2_SCALE = 1.0 / (math.sqrt(HEAD_DIM) * math.log(2.0))
KEY_WIDTH = KV_HEADS * HEAD_DIM
PAIR = HEADS // KV_HEADS * HEAD_DIM
KEY_STEP = 256
VALUE_STEP = 512
NT = (((1,), (1,)), ((), ()))
NN = (((1,), (0,)), ((), ()))


def dot(a, b, dims=NN, precision=None):
    return lax.dot_general(a, b, dims, precision=precision, preferred_element_type=jnp.float32)


def fold_lanes(values, operation):
    folded = values[:, :128]
    for at in range(128, values.shape[1], 128):
        folded = operation(folded, values[:, at:at + 128])
    return folded


def state_of(query_rows, keys, values, mask, count, held):
    rows = query_rows.shape[0]
    widest = None
    for at in range(0, count, KEY_STEP):
        span = min(KEY_STEP, count - at)
        scores = dot(query_rows, keys(at, span), NT)
        if mask is not None:
            scores = jnp.where(mask(at, span), scores, NEG)
        held[:rows, at:at + span] = scores
        folded = fold_lanes(scores, jnp.maximum)
        widest = folded if widest is None else jnp.maximum(widest, folded)
    highest = jnp.maximum(jnp.max(widest, axis=1, keepdims=True) * LOG2_SCALE, LOW)
    totals, summed = None, None
    for at in range(0, count, VALUE_STEP):
        span = min(VALUE_STEP, count - at)
        weights = jnp.exp2(held[:rows, at:at + span] * LOG2_SCALE - highest)
        folded = fold_lanes(weights, jnp.add)
        totals = folded if totals is None else totals + folded
        product = dot(weights.astype(jnp.bfloat16), values(at, span))
        summed = product if summed is None else summed + product
    return highest, jnp.sum(totals, axis=1, keepdims=True), summed


def join(first, second):
    highest = jnp.maximum(first[0], second[0])
    a, b = jnp.exp2(first[0] - highest), jnp.exp2(second[0] - highest)
    return highest, first[1] * a + second[1] * b, first[2] * a + second[2] * b


def stacked(pair):
    return jnp.concatenate([pair[:, :HEAD_DIM], pair[:, HEAD_DIM:]], axis=0)


def fused_kernel(
    n_row, n_col, cap,
    q_ref, suf_ref, leaf_of_ref, parent_ref, leaf_len_ref, branch_len_ref, root_ref, branch_ref, leaf_ref,
    out_ref,
    qg, sbuf, rootb, leafv, branchv, sendq, brq, bro, bst, ret, rst, lm, ll, lo, fo, fs, fin, fins, held,
    load_sem, q_s, q_r, suf_s, suf_r, root_s, root_r, fwd_s, fwd_r, bq_s, bq_r, bo_s, bo_r, bs_s, bs_r,
    f_s, f_r, fs_s, fs_r,
):
    row, col = lax.axis_index("row"), lax.axis_index("col")
    tokens = q_ref.shape[0]
    slots = n_row * cap
    branch_keys, leaf_keys = branchv.shape[0], leafv.shape[0]
    leaf_width = leaf_keys // LEAF_ROW

    def copy_to(src, dst, s, r, **where):
        return pltpu.make_async_remote_copy(
            src_ref=src, dst_ref=dst, send_sem=s, recv_sem=r, device_id=where,
            device_id_type=pl.DeviceIdType.MESH,
        )

    def group(i):
        return (col + i) % 2 + 2 * ((col // 2 + i // 2) % 2)

    def head_lanes(i):
        return pl.ds(pl.multiple_of(group(i) * HEAD_DIM, HEAD_DIM), HEAD_DIM)

    def value_lanes(i):
        return pl.ds(pl.multiple_of(KEY_WIDTH + group(i) * HEAD_DIM, HEAD_DIM), HEAD_DIM)

    loads = []
    for i, (src, dst) in enumerate(((leaf_ref, leafv), (branch_ref, branchv))):
        step = dst.shape[0] // 2
        for j in range(2):
            part = pl.ds(j * step, step)
            loads.append(pltpu.make_async_copy(src.at[part], dst.at[part], load_sem.at[2 * i + j]))
    for load in loads:
        load.start()

    barrier = pltpu.get_barrier_semaphore()
    for k in range(1, n_row):
        pl.semaphore_signal(barrier, inc=1, device_id={"row": (row + k) % n_row},
                            device_id_type=pl.DeviceIdType.MESH)
    for k in range(1, n_col):
        pl.semaphore_signal(barrier, inc=1, device_id={"col": (col + k) % n_col},
                            device_id_type=pl.DeviceIdType.MESH)

    def eye(n):
        return lax.broadcasted_iota(jnp.int32, (n, n), 0) == lax.broadcasted_iota(jnp.int32, (n, n), 1)

    def to_column(values):
        return jnp.sum(jnp.where(eye(values.shape[1]), values, 0.0), axis=1, keepdims=True)

    def to_row(values):
        return jnp.sum(jnp.where(eye(values.shape[0]), values, 0.0), axis=0, keepdims=True)

    leaf_row = leaf_of_ref[...].astype(jnp.float32)
    leaf_col = to_column(leaf_row)
    parent_row = parent_ref[...].astype(jnp.float32)
    leaf_iota = lax.broadcasted_iota(jnp.int32, (tokens, LEAF_ROW), 1).astype(jnp.float32)
    node_col = jnp.sum(jnp.where(leaf_col == leaf_iota, parent_row, 0.0), axis=1, keepdims=True)
    node_row = to_row(node_col)
    above = lax.broadcasted_iota(jnp.int32, (tokens, tokens), 0)
    along = lax.broadcasted_iota(jnp.int32, (tokens, tokens), 1)
    earlier = jnp.where((node_col == node_row) & (along < above), 1.0, 0.0)
    rank_col = jnp.sum(earlier, axis=1, keepdims=True)
    slot_row = to_row(node_col * cap + rank_col)
    spread = jnp.where(
        lax.broadcasted_iota(jnp.int32, (slots, tokens), 0).astype(jnp.float32) == slot_row, 1.0, 0.0
    ).astype(jnp.bfloat16)

    def spread_out(i, pair):
        sendq[i] = dot(spread, pair).astype(jnp.bfloat16).reshape(n_row, cap, PAIR)

    qg[0] = q_ref[...]
    spread_out(0, q_ref[...])
    pl.semaphore_wait(barrier, n_row + n_col - 2)

    sent = []

    def send(copy):
        copy.start()
        sent.append(copy)
        return copy

    def q_copy(i):
        return copy_to(q_ref, qg.at[i], q_s.at[i], q_r.at[i], col=group(i))

    def branch_query(i, k):
        peer = (row + k) % n_row
        return copy_to(sendq.at[i, peer], brq.at[i, row], bq_s.at[i, k], bq_r.at[i, k], row=peer)

    def branch_out(i, k):
        peer = (row + k) % n_row
        return (
            copy_to(bro.at[i, peer], ret.at[i, row], bo_s.at[i, k], bo_r.at[i, k], row=peer),
            copy_to(bst.at[i, peer], rst.at[i, row], bs_s.at[i, k], bs_r.at[i, k], row=peer),
        )

    for i in range(1, n_col):
        send(q_copy(i))
    for k in range(1, n_row):
        branch_query(0, k).start()

    def flip(bit):
        return row + bit - 2 * bit * ((row // bit) % 2)

    mate, beside, below = flip(1), flip(2), flip(4)
    mate_copy = send(copy_to(root_ref, rootb.at[1], root_s.at[0], root_r.at[0], row=mate))
    beside_copy = send(copy_to(root_ref, rootb.at[2], root_s.at[1], root_r.at[1], row=beside))
    below_copy = send(copy_to(root_ref, rootb.at[4], root_s.at[2], root_r.at[2], row=below))
    rootb[0] = root_ref[...]

    first = 2 * (col % 2)

    def suffix_copy(h):
        return copy_to(suf_ref.at[:, pl.ds(h * HEAD_DIM, HEAD_DIM)], sbuf.at[col // 2], suf_s.at[h],
                       suf_r.at[col // 2], col=first + h)

    len_col = to_column(leaf_len_ref[...].astype(jnp.float32))
    key_at = lax.broadcasted_iota(jnp.int32, (1, leaf_keys), 1)
    key_leaf = (key_at // leaf_width).astype(jnp.float32)
    key_place = (col * leaf_width + key_at % leaf_width).astype(jnp.float32)
    rows32 = lax.broadcasted_iota(jnp.int32, (LEAF_ROW, leaf_keys), 0).astype(jnp.float32)
    key_len = jnp.sum(jnp.where(rows32 == key_leaf, len_col, 0.0), axis=0, keepdims=True)
    key_leaf = jnp.where(key_place < key_len, key_leaf, -1.0)
    leaf_col2 = jnp.concatenate([leaf_col, leaf_col], axis=0)

    loads[0].wait()
    loads[1].wait()

    brq[0, row] = sendq[0, row]

    def leaf_level(i):
        rows = stacked(qg[i])
        lm[i], ll[i], lo[i] = state_of(
            rows,
            lambda at, span: leafv[at:at + span, head_lanes(i)],
            lambda at, span: leafv[at:at + span, value_lanes(i)],
            lambda at, span: leaf_col2 == key_leaf[:, at:at + span],
            leaf_keys, held,
        )

    def arrive(i):
        q_copy(i).wait_recv()
        spread_out(i, qg[i])
        for k in range(1, n_row):
            branch_query(i, k).start()
        brq[i, row] = sendq[i, row]

    def leaf_and_next(i, carry):
        leaf_level(i)
        arrive(i + 1)
        return carry

    lax.fori_loop(0, n_col - 2, leaf_and_next, 0)

    loads[2].wait()
    loads[3].wait()
    slot_at = lax.broadcasted_iota(jnp.int32, (n_row, cap, 128), 1)
    lane_at = lax.broadcasted_iota(jnp.int32, (n_row, cap, 128), 2)

    def branch_level(i, carry):
        for k in range(1, n_row):
            branch_query(i, k).wait_recv()
        rows = stacked(brq[i].reshape(slots, PAIR))

        def usable(at, span):
            place = col * branch_keys + at + lax.broadcasted_iota(jnp.int32, (1, span), 1)
            return place < branch_len_ref[...]

        highest, totals, summed = state_of(
            rows,
            lambda at, span: branchv[at:at + span, head_lanes(i)],
            lambda at, span: branchv[at:at + span, value_lanes(i)],
            usable, branch_keys, held,
        )
        for j in range(2):
            for at, column in ((j, highest), (2 + j, totals)):
                column = jnp.broadcast_to(column[j * slots:(j + 1) * slots], (slots, 128))
                line = jnp.sum(
                    jnp.where(slot_at == lane_at, column.reshape(n_row, cap, 128), 0.0), axis=1, keepdims=True
                )
                bst[i, :, at:at + 1, :] = line
                bst[i, :, at + 4:at + 5, :] = line
        summed = jnp.concatenate([summed[:slots], summed[slots:]], axis=1).astype(jnp.bfloat16)
        bro[i] = summed.reshape(n_row, cap, PAIR)
        for k in range(1, n_row):
            for copy in branch_out(i, k):
                copy.start()
        return carry

    branch_level(0, 0)
    arrive(n_col - 1)
    half = root_ref.shape[0] // 2
    beside_copy.wait_recv()
    below_copy.wait_recv()
    low_copy = send(copy_to(rootb.at[2, pl.ds(0, half)], rootb.at[6, pl.ds(0, half)], fwd_s.at[0],
                            fwd_r.at[0], row=below))
    high_copy = send(copy_to(rootb.at[4, pl.ds(half, half)], rootb.at[6, pl.ds(half, half)], fwd_s.at[1],
                             fwd_r.at[1], row=beside))
    shared = [
        send(copy_to(rootb.at[2], rootb.at[3], fwd_s.at[2], fwd_r.at[2], row=mate)),
        send(copy_to(rootb.at[4], rootb.at[5], fwd_s.at[3], fwd_r.at[3], row=mate)),
    ]
    for h in range(2):
        @pl.when(first + h != col)
        def _():
            suffix_copy(h).start()

        @pl.when(first + h == col)
        def _():
            sbuf[col // 2] = suf_ref[:, h * HEAD_DIM:(h + 1) * HEAD_DIM]

    lax.fori_loop(1, n_col - 1, branch_level, 0)

    low_copy.wait_recv()
    high_copy.wait_recv()
    last = send(copy_to(rootb.at[6], rootb.at[7], fwd_s.at[4], fwd_r.at[4], row=mate))
    branch_level(n_col - 1, 0)
    for i in range(n_col):
        ret[i, row] = bro[i, row]
        rst[i, row] = bst[i, row]

    mate_copy.wait_recv()
    for copy in shared:
        copy.wait_recv()
    last.wait_recv()

    def root_level(i, blocks):
        size = root_ref.shape[0]

        def part(lanes):
            def take(at, span):
                chosen = slice(blocks.start + at // size, blocks.start + (at + span) // size)
                return rootb[chosen, :, lanes].reshape(span, HEAD_DIM)
            return take

        state = state_of(
            stacked(qg[i]), part(head_lanes(i)), part(value_lanes(i)), None,
            (blocks.stop - blocks.start) * size, held,
        )
        lm[i], ll[i], lo[i] = join((lm[i], ll[i], lo[i]), state)

    for i, local in ((0, 0), (1, n_col - 1)):
        @pl.when(col != local)
        def _():
            copy_to(suf_ref.at[:, pl.ds(0, HEAD_DIM)], sbuf.at[i], suf_s.at[0], suf_r.at[i],
                    col=(col + 1) % n_col).wait_recv()
    mask = (leaf_col2 == leaf_row) & (
        lax.broadcasted_iota(jnp.int32, (2 * tokens, tokens), 1)
        <= lax.broadcasted_iota(jnp.int32, (2 * tokens, tokens), 0) % tokens
    )
    own_state = state_of(
        stacked(q_ref[...]), lambda at, span: sbuf[0], lambda at, span: sbuf[1], lambda at, span: mask,
        tokens, held,
    )
    lm[0], ll[0], lo[0] = join((lm[0], ll[0], lo[0]), own_state)

    collect = jnp.where(
        lax.broadcasted_iota(jnp.int32, (tokens, slots), 1).astype(jnp.float32) == node_col * cap + rank_col,
        1.0, 0.0,
    ).astype(jnp.bfloat16)
    rank_here = along.astype(jnp.float32) == rank_col

    def final_copies(i):
        return (
            copy_to(fo.at[i], fin.at[i], f_s.at[i], f_r.at[i], col=group(i)),
            copy_to(fs.at[i], fins.at[i], fs_s.at[i], fs_r.at[i], col=group(i)),
        )

    def come_back(step, carry):
        i = (step + 1) % n_col

        @pl.when(i >= n_col - 2)
        def _():
            leaf_level(i)

        root_level(i, slice(0, n_row))
        for k in range(1, n_row):
            for copy in branch_out(i, k):
                copy.wait_recv()
        back = dot(collect, ret[i].reshape(slots, PAIR))
        stats = rst[i]

        def pick(index):
            found = jnp.zeros((tokens, 128), jnp.float32)
            for n in range(n_row):
                found = jnp.where(node_col == n, stats[n, index:index + 1, :], found)
            return jnp.sum(jnp.where(rank_here, found, 0.0), axis=1, keepdims=True)

        summed, lines = [], []
        for j in range(2):
            part = slice(j * tokens, (j + 1) * tokens)
            state = join(
                (lm[i, part], ll[i, part], lo[i, part]),
                (pick(j), pick(2 + j), back[:, j * HEAD_DIM:(j + 1) * HEAD_DIM]),
            )
            summed.append(state[2])
            lines += [to_row(state[0]), to_row(state[1])]
        fo[i] = jnp.concatenate(summed, axis=1).astype(jnp.bfloat16)
        fs[i] = jnp.concatenate(lines + lines, axis=0)

        @pl.when(i > 0)
        def _():
            for copy in final_copies(i):
                copy.start()

        return carry

    lax.fori_loop(0, n_col, come_back, 0)
    fin[0] = fo[0]
    fins[0] = fs[0]
    for i in range(1, n_col):
        for copy in final_copies(i):
            copy.wait_recv()
    for j in range(2):
        mine = None
        for i in range(n_col):
            lines = fins[i]
            other = (
                to_column(lines[2 * j:2 * j + 1]), to_column(lines[2 * j + 1:2 * j + 2]),
                fin[i, :, j * HEAD_DIM:(j + 1) * HEAD_DIM].astype(jnp.float32),
            )
            mine = other if mine is None else join(mine, other)
        out_ref[:, j * HEAD_DIM:(j + 1) * HEAD_DIM] = (mine[2] / mine[1]).astype(out_ref.dtype)

    for copy in sent:
        copy.wait_send()
    for h in range(2):
        @pl.when(first + h != col)
        def _():
            suffix_copy(h).wait_send()

    def drain(i, carry):
        for k in range(1, n_row):
            branch_query(i, k).wait_send()
            for copy in branch_out(i, k):
                copy.wait_send()

        @pl.when(i > 0)
        def _():
            for copy in final_copies(i):
                copy.wait_send()

        return carry

    lax.fori_loop(0, n_col, drain, 0)


def on_device_fused(
    queries, suffix_cache, suffix_leaf, leaf_parent, root_cache, branch_cache, branch_length, leaf_cache,
    leaf_length,
):
    n_row, n_col = lax.axis_size("row"), lax.axis_size("col")
    tokens = queries.shape[0]
    cap = tokens // 16 * (LEAF_ROW // n_row)
    slots = n_row * cap
    width = branch_cache.shape[2]
    branch = branch_cache.reshape(-1, width)
    leaf = leaf_cache.reshape(-1, width)
    bf16, f32 = jnp.bfloat16, jnp.float32
    dma = pltpu.SemaphoreType.DMA
    vmem = pltpu.VMEM
    scratch = [
        vmem((n_col, tokens, PAIR), bf16),
        vmem((2, tokens, HEAD_DIM), bf16),
        vmem((n_row,) + root_cache.shape, bf16),
        vmem(leaf.shape, bf16),
        vmem(branch.shape, bf16),
        vmem((n_col, n_row, cap, PAIR), bf16),
        vmem((n_col, n_row, cap, PAIR), bf16),
        vmem((n_col, n_row, cap, PAIR), bf16),
        vmem((n_col, n_row, 8, 128), f32),
        vmem((n_col, n_row, cap, PAIR), bf16),
        vmem((n_col, n_row, 8, 128), f32),
        vmem((KV_HEADS, 2 * tokens, 1), f32),
        vmem((KV_HEADS, 2 * tokens, 1), f32),
        vmem((KV_HEADS, 2 * tokens, HEAD_DIM), f32),
        vmem((KV_HEADS, tokens, PAIR), bf16),
        vmem((KV_HEADS, 8, tokens), f32),
        vmem((n_col, tokens, PAIR), bf16),
        vmem((n_col, 8, tokens), f32),
        vmem((max(2 * slots, 2 * tokens), max(branch.shape[0], leaf.shape[0])), f32),
        dma((4,)),
        dma((n_col,)), dma((n_col,)),
        dma((2,)), dma((2,)),
        dma((3,)), dma((3,)),
        dma((5,)), dma((5,)),
        dma((n_col, n_row)), dma((n_col, n_row)),
        dma((n_col, n_row)), dma((n_col, n_row)),
        dma((n_col, n_row)), dma((n_col, n_row)),
        dma((n_col,)), dma((n_col,)),
        dma((n_col,)), dma((n_col,)),
    ]
    in_vmem = pl.BlockSpec(memory_space=pltpu.VMEM)
    anywhere = pl.BlockSpec(memory_space=pl.ANY)
    return pl.pallas_call(
        functools.partial(fused_kernel, n_row, n_col, cap),
        out_shape=jax.ShapeDtypeStruct(queries.shape, queries.dtype),
        in_specs=[in_vmem] * 7 + [anywhere] * 2,
        out_specs=in_vmem,
        scratch_shapes=scratch,
        compiler_params=pltpu.CompilerParams(
            collective_id=0, has_side_effects=True, vmem_limit_bytes=56 * 2**20
        ),
    )(
        queries, suffix_cache, suffix_leaf, leaf_parent, leaf_length.reshape(1, -1),
        branch_length.reshape(1, 1), root_cache, branch, leaf,
    )


def solution(mesh):
    in_specs = (
        P("row", "col"),
        P("row", "col"),
        P("row", None),
        P("row", None),
        P(("row", "col"), None),
        P("row", "col", None),
        P("row"),
        P("row", "col", None),
        P("row"),
    )
    out_specs = P("row", "col")
    sizes = dict(mesh.shape)
    body = on_device_fused if (sizes["row"], sizes["col"]) == (8, 4) else on_device
    return jax.shard_map(
        body, mesh=mesh, in_specs=in_specs, out_specs=out_specs, check_vma=False
    )
```
